32 devices in a mesh: sec: 4 (over z), lat: 2 (over x), lon: 4 (over y, core).
Axes of the slice: x: 2, y: 2, z: 4, core: 2. Of those that a mesh axis runs over, the one named last changes fastest.
Arguments:
- state: float32 [4, 75, 8, 512], P('sec', None, 'lat', 'lon'), may hold values from -6 to 6
- mixing: bfloat16 [4, 75, 8, 512], P('sec', None, 'lat', 'lon'), may hold values from 0.05 to 50
- eastward: bfloat16 [4, 75, 8, 512], P('sec', None, 'lat', 'lon'), may hold values from -0.44921875 to 0.44921875
- northward: bfloat16 [4, 75, 8, 512], P('sec', None, 'lat', 'lon'), may hold values from -0.44921875 to 0.44921875
- sea_mask: int32 [8, 512], P('lat', 'lon'), may hold values 0 or 1
- weights: bfloat16 [4, 2, 4, 16, 16, 32], P('sec', 'lat', 'lon'), may hold values from -1.5 to 1.5
- source_block: int32 [4, 2, 4, 8, 4], P('sec', 'lat', 'lon'), may hold values from 0 to 31
- dest_block: int32 [4, 2, 4, 8, 4], P('sec', 'lat', 'lon'), may hold values from 0 to 31
- record_counts: int32 [4, 2, 4, 8], P('sec', 'lat', 'lon'), may hold values from 0 to 4, as said below
Outputs:
- adjoint: float32 [4, 75, 8, 512], P('sec', None, 'lat', 'lon')
The draws below stay inside these ranges and needn't reach their ends.
Inputs may be any that keep to these rules, and one draw needn't show every extreme that they name: `record_counts`: in every section some receiving device has 4 live slots from every sending device.
All inputs are finite; a program needn't handle non-finite values. No bound on the sum of `sea_mask` on one device may be relied on, other than what follows from the above.
Results may differ from the reference program's by a relative error of at most 0.0003.
Values sent between devices are 32-bit elements; how exact they have to be, the bound alone decides.
A program may use at most 64 MiB of HBM per device.

```python
import math
import jax
import jax.numpy as jnp
from jax import lax

LEV = 75
CY = 4
CX = 128
BLK = 16
CAP = 4
NCPL = 4
NSUB = 2
NY = 8
NX = 512
PEERS = 8
SLOTS = 32
NBLK = 32
N_SEC = 4
N_LAT = 2
N_LON = 4


def draw_record_counts(key, part):
    drawn_counts = jax.random.randint(key, (N_SEC, N_LAT, N_LON, PEERS), 0, CAP + 1)
    chosen = jax.random.randint(jax.random.fold_in(key, 7), (N_SEC, 1, 1, 1), 0, N_LAT * N_LON)
    receiver_index = (jnp.arange(N_LAT, dtype=jnp.int32)[:, None] * N_LON + jnp.arange(N_LON, dtype=jnp.int32)[None, :])[None, :, :, None]
    return jnp.where(receiver_index == chosen, CAP, drawn_counts).astype(jnp.int32)


def draw_mixing(key, part):
    column_key = jax.random.fold_in(key, 11)
    level_key = jax.random.fold_in(key, 13)
    lower_log = math.log(0.05)
    upper_log = math.log(50.0)
    column_base = jnp.exp(jax.random.uniform(column_key, (N_SEC, 1, NY, NX), jnp.float32, minval=lower_log, maxval=upper_log))
    level_factor = jnp.exp(jax.random.uniform(level_key, (N_SEC, LEV, NY, NX), jnp.float32, minval=-0.7, maxval=0.7))
    return jnp.clip(column_base * level_factor, 0.05, 50.0).astype(jnp.bfloat16)


def touch_ends(values, key, least, high):
    longest = values.shape.index(max(values.shape))
    spots = []
    for shift in (0, 1):
        where = [jax.random.randint(jax.random.fold_in(key, axis), (), 0, length) for axis, length in enumerate(values.shape)]
        where[longest] = (where[longest] + shift) % values.shape[longest]
        spots.append(tuple(where))
    return values.at[spots[0]].set(least).at[spots[1]].set(high)


def level_of(own_key, shape, shards, low, largest):
    factor_of, own = 1.0, jax.random.fold_in(own_key, 6)
    for position, parts in shards:
        steps = jnp.exp(jax.random.uniform(jax.random.fold_in(own, position), (parts,), jnp.float32, low / len(shards), largest / len(shards)))
        factor_of = factor_of * jnp.repeat(steps, shape[position] // parts).reshape([-1 if axis == position else 1 for axis in range(len(shape))])
    return factor_of


def centred(own_key, shape, deviation, most, shards=(), held_as=jnp.bfloat16):
    result = deviation * jax.random.normal(own_key, shape, jnp.float32)
    if shards:
        result = result * level_of(own_key, shape, shards, -0.22, 0.18)
    return jnp.clip(result, -most, most).astype(held_as)


def setup_inputs(seed: int = 0) -> dict:
    seeds = jax.random.split(jax.random.key(seed), 10)
    state = centred(seeds[0], (N_SEC, LEV, NY, NX), 1.0, 6.0, ((0, 4), (2, 2), (3, 4)), jnp.float32)
    mixing = draw_mixing(jax.random.fold_in(seeds[9], 71), 0)
    eastward = jnp.clip(jax.random.uniform(seeds[2], (N_SEC, LEV, NY, NX), jnp.float32, -0.44921875, 0.44921875) * level_of(seeds[2], (N_SEC, LEV, NY, NX), ((0, 4), (2, 2), (3, 4)), -0.4, 0.0), -0.44921875, 0.44921875).astype(jnp.bfloat16)
    northward = jnp.clip(jax.random.uniform(seeds[3], (N_SEC, LEV, NY, NX), jnp.float32, -0.44921875, 0.44921875) * level_of(seeds[3], (N_SEC, LEV, NY, NX), ((0, 4), (2, 2), (3, 4)), -0.4, 0.0), -0.44921875, 0.44921875).astype(jnp.bfloat16)
    sea_mask = touch_ends((jax.random.randint(seeds[4], (NY, NX), 0, 10) < 7).astype(jnp.int32), jax.random.fold_in(seeds[4], 1), 0, 1)
    weights = centred(seeds[5], (N_SEC, N_LAT, N_LON, BLK, BLK, SLOTS), BLK ** -0.5, 1.5, ((0, 4), (1, 2), (2, 4)))
    source_block = touch_ends(jax.random.randint(seeds[6], (N_SEC, N_LAT, N_LON, PEERS, CAP), 0, NBLK), jax.random.fold_in(seeds[6], 1), 0, NBLK - 1).astype(jnp.int32)
    dest_block = touch_ends(jax.random.randint(seeds[7], (N_SEC, N_LAT, N_LON, PEERS, CAP), 0, NBLK), jax.random.fold_in(seeds[7], 1), 0, NBLK - 1).astype(jnp.int32)
    record_counts = draw_record_counts(jax.random.fold_in(seeds[9], 71), 0)
    return dict(state=state, mixing=mixing, eastward=eastward, northward=northward, sea_mask=sea_mask, weights=weights, source_block=source_block, dest_block=dest_block, record_counts=record_counts)


def column_solve(right, coeff):
    zero_row = jnp.zeros_like(coeff[:1])
    lower_band = jnp.concatenate([zero_row, coeff[1:]], axis=0)
    upper_band = jnp.concatenate([coeff[1:], zero_row], axis=0)
    centre = 1.0 + lower_band + upper_band

    def sweep_down(carried, entries):
        prior_c, prior_z = carried
        centre_k, beneath, overhead, right_k = entries
        pivot_value = centre_k + beneath * prior_c
        factor = -overhead / pivot_value
        partial_value = (right_k + beneath * prior_z) / pivot_value
        return (factor, partial_value), (factor, partial_value)

    start_pair = (jnp.zeros_like(right[0]), jnp.zeros_like(right[0]))
    _, (factors, partials) = lax.scan(sweep_down, start_pair, (centre, lower_band, upper_band, right))

    def sweep_up(carried, entries):
        factor, partial_value = entries
        solved_k = partial_value - factor * carried
        return solved_k, solved_k

    _, solved = lax.scan(sweep_up, jnp.zeros_like(right[0]), (factors, partials), reverse=True)
    return solved


def advect(mixed_adj, east_speed, north_speed):
    east_flux = east_speed * mixed_adj
    north_flux = north_speed * mixed_adj
    east_diff = jnp.roll(east_flux, -1, axis=2) - jnp.roll(east_flux, 1, axis=2)
    padded = jnp.pad(north_flux, ((0, 0), (1, 1), (0, 0)))
    north_diff = padded[:, 2:] - padded[:, :-2]
    return mixed_adj + 0.5 * (east_diff + north_diff)


def substep(adjoint, mixing, eastward, northward, keep):
    def section_step(entries):
        field_part, mix_part, east_part, north_part, keep_part = entries
        mixed_adj = column_solve(field_part, mix_part.astype(jnp.float32))
        return advect(mixed_adj, east_part.astype(jnp.float32), north_part.astype(jnp.float32)) * keep_part
    return lax.map(section_step, (adjoint, mixing, eastward, northward, keep))


def couple(adjoint, weight_table, source_block, dest_block, record_counts):
    section_count = adjoint.shape[0]
    peer_count = N_LAT * N_LON
    surface = adjoint[:, LEV - 1].reshape(section_count, N_LAT, CY, N_LON, CX)
    surface = surface.transpose(0, 1, 3, 2, 4).reshape(section_count, N_LAT, N_LON, NBLK, BLK)
    sources = source_block.reshape(section_count, N_LAT, N_LON, SLOTS)
    gathered = jnp.take_along_axis(surface, sources[..., None], axis=3)
    contribution = jnp.einsum("saodiz,saozi->saodz", weight_table, gathered, precision=lax.Precision.HIGHEST)
    outgoing = contribution.reshape(section_count, peer_count, BLK, peer_count, CAP)
    arrived = outgoing.transpose(0, 3, 1, 4, 2)
    counts_view = record_counts.reshape(section_count, peer_count, peer_count)
    live_slot = jnp.arange(CAP, dtype=jnp.int32)[None, None, None, :] < counts_view[..., None]
    air_mask = (jnp.arange(section_count, dtype=jnp.int32) < section_count - 1)[:, None, None, None]
    arrived_live = arrived * jnp.logical_and(live_slot, air_mask)[..., None].astype(jnp.float32)
    receiver_ids = jnp.arange(section_count * peer_count, dtype=jnp.int32).reshape(section_count, peer_count, 1, 1)
    segment_ids = receiver_ids * NBLK + dest_block.reshape(section_count, peer_count, peer_count, CAP).astype(jnp.int32)
    accumulated = jax.ops.segment_sum(arrived_live.reshape(-1, BLK), segment_ids.reshape(-1),
                                      num_segments=section_count * peer_count * NBLK)
    accumulated = accumulated.reshape(section_count, peer_count, NBLK, BLK).sum(axis=0)
    forcing = accumulated.reshape(N_LAT, N_LON, CY, CX).transpose(0, 2, 1, 3).reshape(NY, NX)
    return forcing


def reference(state, mixing, eastward, northward, sea_mask, weights, source_block, dest_block, record_counts):
    section_count = state.shape[0]
    ocean_keep = sea_mask.astype(jnp.float32)
    keep = jnp.concatenate([jnp.ones((section_count - 1, NY, NX), jnp.float32), ocean_keep[None]], axis=0)
    weight_table = weights.astype(jnp.float32)
    adjoint = state
    for coupling in range(NCPL):
        for repeat in range(NSUB):
            adjoint = substep(adjoint, mixing, eastward, northward, keep)
        forcing = couple(adjoint, weight_table, source_block, dest_block, record_counts)
        adjoint = adjoint.at[section_count - 1, 0].add(forcing * ocean_keep)
    return adjoint
```

```python
import functools

import jax
import jax.numpy as jnp
from jax import lax
from jax.experimental import pallas as pl
from jax.experimental.pallas import tpu as pltpu
from jax.sharding import PartitionSpec as P

NCPL = 4
NSUB = 2
MESH = pl.DeviceIdType.MESH
F32 = jnp.float32


def window(
    n_sec, n_lat, n_lon, cap, state, mixing, eastward, northward, sea, weights, source, dest, counts,
    out, fld, loc, coef, inv, low, east, north, ew_out, ew_in, ns_out, ns_in, table, rows_of,
    contrib, arrived, dest_out, dest_in, ew_send, ew_recv, ns_send, ns_recv, c_send, c_recv,
    d_send, d_recv,
):
    lev, cy, cx = state.shape
    half = lev // 2
    blk = weights.shape[0]
    slots = weights.shape[2]
    peers = n_lat * n_lon
    per_row = cx // blk
    groups = ns_out.shape[2]
    total = NCPL * NSUB

    s, a, o = lax.axis_index("sec"), lax.axis_index("lat"), lax.axis_index("lon")
    me = a * n_lon + o
    ocean = n_sec - 1
    is_ocean = s == ocean
    is_air = s != ocean
    to_east = (s, a, lax.rem(o + 1, n_lon))
    to_west = (s, a, lax.rem(o + n_lon - 1, n_lon))
    to_north = (s, a + 1, o)
    to_south = (s, a - 1, o)
    has_north = a < n_lat - 1
    has_south = a > 0

    barrier = pltpu.get_barrier_semaphore()

    def greet(target):
        pl.semaphore_signal(barrier, inc=1, device_id=target, device_id_type=MESH)

    greet(to_east)
    greet(to_west)

    @pl.when(has_north)
    def _():
        greet(to_north)

    @pl.when(has_south)
    def _():
        greet(to_south)

    @pl.when(is_ocean)
    def _():
        def each(q, carry):
            for sec in range(n_sec - 1):
                greet((sec, q // n_lon, q % n_lon))
            return carry

        lax.fori_loop(0, peers, each, 0)

    lane = lax.broadcasted_iota(jnp.int32, (2 * cy, cx), 1)
    sub = lax.broadcasted_iota(jnp.int32, (2 * cy, cx), 0)
    row = sub % cy
    first_row, last_row = row == 0, row == cy - 1
    first_lane, last_lane = lane == 0, lane == cx - 1
    zero = jnp.zeros((2 * cy, cx), F32)

    def pair(ref, upper, lower):
        return jnp.concatenate([ref[upper].astype(F32), ref[lower].astype(F32)], axis=0)

    mask4 = sea[...].astype(F32)
    mask8 = jnp.concatenate([mask4, mask4], axis=0)
    keep = jnp.where(is_ocean, mask8, jnp.ones_like(mask8))

    for k in range(half + 1):
        fld[k] = pair(state, k, lev - 1 - k)
        east[k] = 0.5 * pair(eastward, k, lev - 1 - k)
        north[k] = 0.5 * pair(northward, k, lev - 1 - k)

    outer = zero
    held = zero
    for k in range(half):
        inner = pair(mixing, k + 1, lev - 1 - k)
        grown = 1.0 + outer * held
        inverse = 1.0 / (grown + inner)
        inv[k] = inverse
        low[k] = outer * inverse
        coef[k] = inner * inverse
        held = grown * inverse
        outer = inner
    joined = outer * held
    inv[half] = 1.0 / (1.0 + joined + pltpu.roll(joined, cy, 0))
    low[half] = outer

    @pl.when(jnp.logical_not(has_north))
    def _():
        ns_in[:, 0] = jnp.zeros((total, groups, 2 * cy, cx), F32)

    @pl.when(jnp.logical_not(has_south))
    def _():
        ns_in[:, 1] = jnp.zeros((total, groups, 2 * cy, cx), F32)

    lane_s = lax.broadcasted_iota(jnp.int32, (slots, cx), 1)

    @pl.when(is_air)
    def _():
        lane1 = lax.broadcasted_iota(jnp.int32, (1, cx), 1)
        for z in range(slots):
            rows_of[z : z + 1, :] = jnp.full((1, cx), source[z // cap, z % cap], jnp.int32)
        blocks = rows_of[...]
        here = (lane_s // blk) == (blocks % per_row)
        rows_of[...] = blocks // per_row
        spread = (
            lax.broadcasted_iota(jnp.int32, (blk, cx), 1) % blk
            == lax.broadcasted_iota(jnp.int32, (blk, cx), 0)
        ).astype(F32).astype(jnp.bfloat16)
        for d in range(blk):
            wide = lax.dot_general(
                weights[d], spread, (((0,), (0,)), ((), ())), preferred_element_type=F32
            )
            table[d] = jnp.where(here, wide, 0.0)
        slot_row = lax.broadcasted_iota(jnp.int32, (cap, cx), 0)
        for q in range(peers):
            value = jnp.full((cap, cx), dest[q, 0], jnp.int32)
            for j in range(1, cap):
                value = jnp.where(slot_row == j, dest[q, j], value)
            dest_out[q] = jnp.where(slot_row < counts[0, q], value, -1)

    waits = 2 + has_north.astype(jnp.int32) + has_south.astype(jnp.int32)
    waits = waits + jnp.where(is_air, peers, 0)
    pl.semaphore_wait(barrier, waits)

    def dest_copy(sec):
        return pltpu.make_async_remote_copy(
            src_ref=dest_out, dst_ref=dest_in.at[sec], send_sem=d_send, recv_sem=d_recv.at[sec],
            device_id=(ocean, a, o), device_id_type=MESH,
        )

    @pl.when(is_air)
    def _():
        dest_copy(s).start()

    def ew_copy(t, way):
        return pltpu.make_async_remote_copy(
            src_ref=ew_out.at[t], dst_ref=ew_in.at[t, way], send_sem=ew_send.at[t, way],
            recv_sem=ew_recv.at[t, way], device_id=(to_west, to_east)[way], device_id_type=MESH,
        )

    def ns_copy(t, way):
        return pltpu.make_async_remote_copy(
            src_ref=ns_out.at[t, way], dst_ref=ns_in.at[t, way], send_sem=ns_send.at[t, way],
            recv_sem=ns_recv.at[t, way], device_id=(to_south, to_north)[way], device_id_type=MESH,
        )

    def substep(right, t):
        partial = []
        running = None
        for k in range(half):
            scaled = right[k] * inv[k]
            running = scaled if k == 0 else scaled + low[k] * running
            partial.append(running)
        meet = low[half] * running
        solved = [None] * (half + 1)
        solved[half] = (right[half] + (meet + pltpu.roll(meet, cy, 0))) * inv[half]
        for k in reversed(range(half)):
            solved[k] = partial[k] + coef[k] * solved[k + 1]

        packed = zero
        southward = [zero] * groups
        northbound = [zero] * groups
        for k in reversed(range(half + 1)):
            flux = north[k] * solved[k]
            g, j = k // cy, k % cy
            here = row == j
            down = flux if j == 0 else pltpu.roll(flux, j, 0)
            up = flux if j == cy - 1 else pltpu.roll(flux, j + cy + 1, 0)
            southward[g] = jnp.where(here, down, southward[g])
            northbound[g] = jnp.where(here, up, northbound[g])
            if j == 0:
                ns_out[t, 0, g] = southward[g]
                ns_out[t, 1, g] = northbound[g]

        @pl.when(has_south)
        def _():
            ns_copy(t, 0).start()

        @pl.when(has_north)
        def _():
            ns_copy(t, 1).start()

        for k in range(half + 1):
            flux = east[k] * solved[k]
            packed = jnp.where((lane // 2) == k, pltpu.roll(flux, 2 * k + 1, 1), packed)
        ew_out[t] = packed
        ew_copy(t, 0).start()
        ew_copy(t, 1).start()

        for k in range(half + 1):
            flux = east[k] * solved[k]
            across = jnp.where(last_lane, 0.0, pltpu.roll(flux, cx - 1, 1)) - jnp.where(
                first_lane, 0.0, pltpu.roll(flux, 1, 1)
            )
            flux = north[k] * solved[k]
            along = jnp.where(last_row, 0.0, pltpu.roll(flux, 2 * cy - 1, 0)) - jnp.where(
                first_row, 0.0, pltpu.roll(flux, 1, 0)
            )
            loc[k] = solved[k] + (across + along)

        ew_copy(t, 0).wait_recv()
        ew_copy(t, 1).wait_recv()

        @pl.when(has_north)
        def _():
            ns_copy(t, 0).wait_recv()

        @pl.when(has_south)
        def _():
            ns_copy(t, 1).wait_recv()

        from_east, from_west = ew_in[t, 0], ew_in[t, 1]
        sides = jnp.where(
            lane % 2 == 0, pltpu.roll(from_east, cx - 1, 1), -pltpu.roll(from_west, 1, 1)
        )
        edge = jnp.logical_or(first_lane, last_lane)
        result = []
        for k in range(half + 1):
            g, j = k // cy, k % cy
            beside = jnp.where(edge, pltpu.roll(sides, cx - (2 * k + 1), 1), 0.0)
            above, below = ns_in[t, 0, g], ns_in[t, 1, g]
            if j != cy - 1:
                above = pltpu.roll(above, cy - 1 - j, 0)
            if j != 0:
                below = pltpu.roll(below, 2 * cy - j, 0)
            beyond = jnp.where(last_row, above, jnp.where(first_row, -below, 0.0))
            result.append((loc[k] + (beside + beyond)) * keep)
        return result

    def contrib_copy(c, p):
        return pltpu.make_async_remote_copy(
            src_ref=contrib.at[c, p], dst_ref=arrived.at[c, jnp.minimum(s, ocean - 1), me],
            send_sem=c_send.at[c], recv_sem=c_recv.at[c],
            device_id=(ocean, p // n_lon, p % n_lon), device_id_type=MESH,
        )

    @pl.when(is_ocean)
    def _():
        for sec in range(n_sec - 1):
            dest_copy(sec).wait_recv()

    def coupling(c, carry):
        right = [fld[k] for k in range(half + 1)]
        for repeat in range(NSUB):
            right = substep(right, NSUB * c + repeat)
        for k in range(half + 1):
            fld[k] = right[k]

        @pl.when(is_air)
        def _():
            surface = fld[0][cy:, :]
            picked = jnp.zeros((slots, cx), F32)
            for y in range(cy):
                picked = jnp.where(
                    rows_of[...] == y, jnp.broadcast_to(surface[y : y + 1], (slots, cx)), picked
                )
            given = jnp.zeros((slots, cx), F32)
            for d in range(blk):
                value = jnp.sum(picked * table[d], axis=1, keepdims=True)
                given = jnp.where(lane_s % blk == d, value, given)
            for p in range(peers):
                contrib[c, p] = given[p * cap : (p + 1) * cap, :]

            def each(p, carry):
                contrib_copy(c, p).start()
                return carry

            lax.fori_loop(0, peers, each, 0)

        @pl.when(is_ocean)
        def _():
            pltpu.make_async_copy(arrived.at[c], arrived.at[c], c_recv.at[c]).wait()
            group = lax.broadcasted_iota(jnp.int32, (cap, cx), 1) // blk

            def each(q, sums):
                sums = list(sums)
                for sec in range(n_sec - 1):
                    place = dest_in[sec, q] - group
                    value = arrived[c, sec, q]
                    for y in range(cy):
                        sums[y] = sums[y] + jnp.where(place == per_row * y, value, 0.0)
                return tuple(sums)

            start = (jnp.zeros((cap, cx), F32),) * cy
            sums = lax.fori_loop(0, peers, each, start, unroll=8)
            forcing = zero
            for y in range(cy):
                forcing = jnp.where(
                    sub == y, jnp.sum(sums[y], axis=0, keepdims=True), forcing
                )
            fld[0] = fld[0] + forcing * mask8

        return carry

    lax.fori_loop(0, NCPL, coupling, 0)

    for k in range(half):
        value = fld[k]
        out[k] = value[:cy]
        out[lev - 1 - k] = value[cy:]
    out[half] = fld[half][:cy]

    def finish(t, carry):
        ew_copy(t, 0).wait_send()
        ew_copy(t, 1).wait_send()

        @pl.when(has_south)
        def _():
            ns_copy(t, 0).wait_send()

        @pl.when(has_north)
        def _():
            ns_copy(t, 1).wait_send()

        return carry

    lax.fori_loop(0, total, finish, 0)

    @pl.when(is_air)
    def _():
        dest_copy(s).wait_send()

        def done(c, carry):
            pltpu.make_async_copy(contrib.at[c], contrib.at[c], c_send.at[c]).wait()
            return carry

        lax.fori_loop(0, NCPL, done, 0)


def local(
    sizes, state, mixing, eastward, northward, sea_mask, weights, source_block, dest_block,
    record_counts,
):
    n_sec, n_lat, n_lon = sizes
    _, lev, cy, cx = state.shape
    blk, slots = weights.shape[3], weights.shape[5]
    peers, cap = source_block.shape[3:]
    half = lev // 2
    total = NCPL * NSUB
    groups = -(-(half + 1) // cy)
    assert lev % 2 == 1 and 2 * (half + 1) <= cx and cx % blk == 0
    levels = (half + 1, 2 * cy, cx)
    vmem = pl.BlockSpec(memory_space=pltpu.VMEM)
    smem = pl.BlockSpec(memory_space=pltpu.SMEM)
    dma = pltpu.SemaphoreType.DMA
    result = pl.pallas_call(
        functools.partial(window, n_sec, n_lat, n_lon, cap),
        out_shape=jax.ShapeDtypeStruct((lev, cy, cx), F32),
        in_specs=[vmem] * 6 + [smem] * 3,
        out_specs=vmem,
        scratch_shapes=[pltpu.VMEM(levels, F32)] * 7
        + [
            pltpu.VMEM((total, 2 * cy, cx), F32),
            pltpu.VMEM((total, 2, 2 * cy, cx), F32),
            pltpu.VMEM((total, 2, groups, 2 * cy, cx), F32),
            pltpu.VMEM((total, 2, groups, 2 * cy, cx), F32),
            pltpu.VMEM((blk, slots, cx), F32),
            pltpu.VMEM((slots, cx), jnp.int32),
            pltpu.VMEM((NCPL, peers, cap, cx), F32),
            pltpu.VMEM((NCPL, n_sec - 1, peers, cap, cx), F32),
            pltpu.VMEM((peers, cap, cx), jnp.int32),
            pltpu.VMEM((n_sec - 1, peers, cap, cx), jnp.int32),
            dma((total, 2)), dma((total, 2)), dma((total, 2)), dma((total, 2)),
            dma((NCPL,)), dma((NCPL,)), dma, dma((n_sec - 1,)),
        ],
        compiler_params=pltpu.CompilerParams(
            collective_id=0, has_side_effects=True, vmem_limit_bytes=48 * 1024 * 1024
        ),
    )(
        state[0], mixing[0], eastward[0], northward[0], sea_mask, weights[0, 0, 0],
        source_block[0, 0, 0], dest_block[0, 0, 0], record_counts[0, 0],
    )
    return result[None]


def solution(mesh):
    in_specs = (
        P("sec", None, "lat", "lon"),
        P("sec", None, "lat", "lon"),
        P("sec", None, "lat", "lon"),
        P("sec", None, "lat", "lon"),
        P("lat", "lon"),
        P("sec", "lat", "lon", None, None, None),
        P("sec", "lat", "lon", None, None),
        P("sec", "lat", "lon", None, None),
        P("sec", "lat", "lon", None),
    )
    out_specs = P("sec", None, "lat", "lon")
    sizes = tuple(mesh.shape[name] for name in ("sec", "lat", "lon"))
    return jax.shard_map(
        functools.partial(local, sizes), mesh=mesh, in_specs=in_specs, out_specs=out_specs,
        check_vma=False,
    )
```

```python
import functools

import jax
import jax.numpy as jnp
from jax import lax
from jax.experimental import pallas as pl
from jax.experimental.pallas import tpu as pltpu
from jax.sharding import PartitionSpec as P

NCPL = 4
NSUB = 2
MESH = pl.DeviceIdType.MESH
F32 = jnp.float32


def window(
    n_sec, n_lat, n_lon, cap, state_in, mixing_in, eastward_in, northward_in, sea_in, weights_in,
    source_in, dest_in_hbm, counts_in, out, state, mixing, eastward, northward, sea, weights, source,
    dest, counts, load_sem, fld, loc, coef, inv, low, east, north, ew_out, ew_in, ns_out, ns_in, table, rows_of,
    contrib, arrived, dest_out, dest_in, ew_send, ew_recv, ns_send, ns_recv, c_send, c_recv,
    d_send, d_recv,
):
    lev, cy, cx = state.shape
    half = lev // 2
    blk = weights.shape[0]
    slots = weights.shape[2]
    peers = n_lat * n_lon
    per_row = cx // blk
    groups = ns_out.shape[2]
    total = NCPL * NSUB

    s, a, o = lax.axis_index("sec"), lax.axis_index("lat"), lax.axis_index("lon")
    me = a * n_lon + o
    ocean = n_sec - 1
    is_ocean = s == ocean
    is_air = s != ocean
    to_east = (s, a, lax.rem(o + 1, n_lon))
    to_west = (s, a, lax.rem(o + n_lon - 1, n_lon))
    to_north = (s, a + 1, o)
    to_south = (s, a - 1, o)
    has_north = a < n_lat - 1
    has_south = a > 0

    loads = [
        pltpu.make_async_copy(src, dst, load_sem.at[i])
        for i, (src, dst) in enumerate(
            (
                (mixing_in, mixing), (state_in, state), (eastward_in, eastward),
                (northward_in, northward), (sea_in, sea), (weights_in, weights),
                (source_in, source), (dest_in_hbm, dest), (counts_in, counts),
            )
        )
    ]
    for load in loads:
        load.start()

    barrier = pltpu.get_barrier_semaphore()

    def greet(target):
        pl.semaphore_signal(barrier, inc=1, device_id=target, device_id_type=MESH)

    greet(to_east)
    greet(to_west)

    @pl.when(has_north)
    def _():
        greet(to_north)

    @pl.when(has_south)
    def _():
        greet(to_south)

    @pl.when(is_ocean)
    def _():
        def each(q, carry):
            for sec in range(n_sec - 1):
                greet((sec, q // n_lon, q % n_lon))
            return carry

        lax.fori_loop(0, peers, each, 0)

    lane = lax.broadcasted_iota(jnp.int32, (2 * cy, cx), 1)
    sub = lax.broadcasted_iota(jnp.int32, (2 * cy, cx), 0)
    row = sub % cy
    first_row, last_row = row == 0, row == cy - 1
    first_lane, last_lane = lane == 0, lane == cx - 1
    zero = jnp.zeros((2 * cy, cx), F32)

    def pair(ref, upper, lower):
        return jnp.concatenate([ref[upper].astype(F32), ref[lower].astype(F32)], axis=0)

    loads[0].wait()

    outer = zero
    held = zero
    for k in range(half):
        inner = pair(mixing, k + 1, lev - 1 - k)
        grown = 1.0 + outer * held
        inverse = 1.0 / (grown + inner)
        inv[k] = inverse
        low[k] = outer * inverse
        coef[k] = inner * inverse
        held = grown * inverse
        outer = inner
    joined = outer * held
    inv[half] = 1.0 / (1.0 + joined + pltpu.roll(joined, cy, 0))
    low[half] = outer

    for load in loads[1:]:
        load.wait()
    mask4 = sea[...].astype(F32)
    mask8 = jnp.concatenate([mask4, mask4], axis=0)
    keep = jnp.where(is_ocean, mask8, jnp.ones_like(mask8))

    for k in range(half + 1):
        fld[k] = pair(state, k, lev - 1 - k)
        east[k] = 0.5 * pair(eastward, k, lev - 1 - k)
        north[k] = 0.5 * pair(northward, k, lev - 1 - k)

    if n_lat != 2:

        @pl.when(jnp.logical_not(has_north))
        def _():
            ns_in[:, 0] = jnp.zeros((total, groups, 2 * cy, cx), F32)

        @pl.when(jnp.logical_not(has_south))
        def _():
            ns_in[:, 1] = jnp.zeros((total, groups, 2 * cy, cx), F32)

    lane_s = lax.broadcasted_iota(jnp.int32, (slots, cx), 1)

    waits = 2 + has_north.astype(jnp.int32) + has_south.astype(jnp.int32)
    waits = waits + jnp.where(is_air, peers, 0)
    pl.semaphore_wait(barrier, waits)

    def dest_copy(sec):
        return pltpu.make_async_remote_copy(
            src_ref=dest_out, dst_ref=dest_in.at[sec], send_sem=d_send, recv_sem=d_recv.at[sec],
            device_id=(ocean, a, o), device_id_type=MESH,
        )

    def prepare_records():
        lane1 = lax.broadcasted_iota(jnp.int32, (1, cx), 1)
        for z in range(slots):
            rows_of[z : z + 1, :] = jnp.full((1, cx), source[z % cap, z // cap], jnp.int32)
        blocks = rows_of[...]
        here = (lane_s // blk) == (blocks % per_row)
        rows_of[...] = blocks // per_row
        spread = (
            lax.broadcasted_iota(jnp.int32, (blk, cx), 1) % blk
            == lax.broadcasted_iota(jnp.int32, (blk, cx), 0)
        ).astype(F32).astype(jnp.bfloat16)
        for d in range(blk):
            wide = lax.dot_general(
                weights[d], spread, (((0,), (0,)), ((), ())), preferred_element_type=F32
            )
            table[d] = jnp.where(here, wide, 0.0)
        slot_row = lax.broadcasted_iota(jnp.int32, (cap, cx), 0)
        for q in range(peers):
            value = jnp.full((cap, cx), dest[0, q], jnp.int32)
            for j in range(1, cap):
                value = jnp.where(slot_row == j, dest[j, q], value)
            dest_out[q] = jnp.where(slot_row < counts[0, q], value, -1)
        dest_copy(s).start()

    def ew_copy(t, way):
        return pltpu.make_async_remote_copy(
            src_ref=ew_out.at[t], dst_ref=ew_in.at[t, way], send_sem=ew_send.at[t, way],
            recv_sem=ew_recv.at[t, way], device_id=(to_west, to_east)[way], device_id_type=MESH,
        )

    def ns_copy(t, way):
        return pltpu.make_async_remote_copy(
            src_ref=ns_out.at[t, way], dst_ref=ns_in.at[t, way], send_sem=ns_send.at[t, way],
            recv_sem=ns_recv.at[t, way], device_id=(to_south, to_north)[way], device_id_type=MESH,
        )

    def partner_copy(t, piece):
        return pltpu.make_async_remote_copy(
            src_ref=ns_out.at[t, piece], dst_ref=ns_in.at[t, piece], send_sem=ns_send.at[t, piece],
            recv_sem=ns_recv.at[t, piece], device_id=(s, 1 - a, o), device_id_type=MESH,
        )

    facing = (cy - 1) * (1 - a)
    facing_row = row == facing
    facing_sign = jnp.where(a == 0, 1.0, -1.0).astype(F32)

    def substep(right, t, meanwhile):
        partial = []
        running = None
        for k in range(half):
            scaled = right[k] * inv[k]
            running = scaled if k == 0 else scaled + low[k] * running
            partial.append(running)
        meet = low[half] * running
        solved = [None] * (half + 1)
        solved[half] = (right[half] + (meet + pltpu.roll(meet, cy, 0))) * inv[half]
        for k in reversed(range(half)):
            solved[k] = partial[k] + coef[k] * solved[k + 1]

        packed = zero
        if n_lat == 2:
            for k in reversed(range(half + 1)):
                g, j = k // cy, k % cy
                flux = pltpu.roll(
                    north[k] * solved[k], lax.rem(j + 2 * cy - facing, 2 * cy), 0
                )
                group = jnp.where(row == j, flux, zero if k == half or j == cy - 1 else group)
                flux = pltpu.roll(east[k] * solved[k], 2 * k + 1, 1)
                packed = jnp.where((lane // 2) == k, flux, packed)
                if j == 0:
                    ns_out[t, g // groups, g % groups] = group
                    if g == groups:
                        partner_copy(t, 1).start()
            partner_copy(t, 0).start()
        else:
            southward = [zero] * groups
            northbound = [zero] * groups
            for k in reversed(range(half + 1)):
                flux = north[k] * solved[k]
                g, j = k // cy, k % cy
                here = row == j
                down = flux if j == 0 else pltpu.roll(flux, j, 0)
                up = flux if j == cy - 1 else pltpu.roll(flux, j + cy + 1, 0)
                southward[g] = jnp.where(here, down, southward[g])
                northbound[g] = jnp.where(here, up, northbound[g])
                if j == 0:
                    ns_out[t, 0, g] = southward[g]
                    ns_out[t, 1, g] = northbound[g]

            @pl.when(has_south)
            def _():
                ns_copy(t, 0).start()

            @pl.when(has_north)
            def _():
                ns_copy(t, 1).start()

            for k in range(half + 1):
                flux = pltpu.roll(east[k] * solved[k], 2 * k + 1, 1)
                packed = jnp.where((lane // 2) == k, flux, packed)
        ew_out[t] = packed
        ew_copy(t, 0).start()
        ew_copy(t, 1).start()
        meanwhile()

        for k in range(half + 1):
            flux = east[k] * solved[k]
            across = jnp.where(last_lane, 0.0, pltpu.roll(flux, cx - 1, 1)) - jnp.where(
                first_lane, 0.0, pltpu.roll(flux, 1, 1)
            )
            flux = north[k] * solved[k]
            along = jnp.where(last_row, 0.0, pltpu.roll(flux, 2 * cy - 1, 0)) - jnp.where(
                first_row, 0.0, pltpu.roll(flux, 1, 0)
            )
            loc[k] = solved[k] + (across + along)

        ew_copy(t, 0).wait_recv()
        ew_copy(t, 1).wait_recv()

        if n_lat == 2:
            partner_copy(t, 1).wait_recv()
            partner_copy(t, 0).wait_recv()
        else:

            @pl.when(has_north)
            def _():
                ns_copy(t, 0).wait_recv()

            @pl.when(has_south)
            def _():
                ns_copy(t, 1).wait_recv()

        from_east, from_west = ew_in[t, 0], ew_in[t, 1]
        sides = jnp.where(
            lane % 2 == 0, pltpu.roll(from_east, cx - 1, 1), -pltpu.roll(from_west, 1, 1)
        )
        edge = jnp.logical_or(first_lane, last_lane)
        result = []
        for k in range(half + 1):
            g, j = k // cy, k % cy
            beside = jnp.where(edge, pltpu.roll(sides, cx - (2 * k + 1), 1), 0.0)
            if n_lat == 2:
                if j == 0 or k == 0:
                    group = ns_in[t, g // groups, g % groups] * facing_sign
                beyond = pltpu.roll(group, lax.rem(facing + 2 * cy - j, 2 * cy), 0)
                beyond = jnp.where(facing_row, beyond, 0.0)
            else:
                above, below = ns_in[t, 0, g], ns_in[t, 1, g]
                if j != cy - 1:
                    above = pltpu.roll(above, cy - 1 - j, 0)
                if j != 0:
                    below = pltpu.roll(below, 2 * cy - j, 0)
                beyond = jnp.where(last_row, above, jnp.where(first_row, -below, 0.0))
            result.append((loc[k] + (beside + beyond)) * keep)
        return result

    def contrib_copy(c, p):
        return pltpu.make_async_remote_copy(
            src_ref=contrib.at[c, p], dst_ref=arrived.at[c, jnp.minimum(s, ocean - 1), me],
            send_sem=c_send.at[c], recv_sem=c_recv.at[c],
            device_id=(ocean, p // n_lon, p % n_lon), device_id_type=MESH,
        )

    def nothing():
        pass

    def first_flight(c):
        pl.when(jnp.logical_and(is_air, c == 0))(prepare_records)

    def coupling(c, carry):
        right = [fld[k] for k in range(half + 1)]
        for repeat in range(NSUB):
            right = substep(
                right, NSUB * c + repeat, functools.partial(first_flight, c) if repeat == 0 else nothing
            )
        for k in range(half + 1):
            fld[k] = right[k]

        @pl.when(is_air)
        def _():
            surface = fld[0][cy:, :]
            picked = jnp.zeros((slots, cx), F32)
            for y in range(cy):
                picked = jnp.where(
                    rows_of[...] == y, jnp.broadcast_to(surface[y : y + 1], (slots, cx)), picked
                )
            given = jnp.zeros((slots, cx), F32)
            for d in range(blk):
                value = jnp.sum(picked * table[d], axis=1, keepdims=True)
                given = jnp.where(lane_s % blk == d, value, given)
            for p in range(peers):
                contrib[c, p] = given[p * cap : (p + 1) * cap, :]

            def each(p, carry):
                contrib_copy(c, p).start()
                return carry

            lax.fori_loop(0, peers, each, 0)

        @pl.when(is_ocean)
        def _():
            @pl.when(c == 0)
            def _():
                for sec in range(n_sec - 1):
                    dest_copy(sec).wait_recv()

            pltpu.make_async_copy(arrived.at[c], arrived.at[c], c_recv.at[c]).wait()
            group = lax.broadcasted_iota(jnp.int32, (cap, cx), 1) // blk

            def each(q, sums):
                sums = list(sums)
                for sec in range(n_sec - 1):
                    place = dest_in[sec, q] - group
                    value = arrived[c, sec, q]
                    for y in range(cy):
                        sums[y] = sums[y] + jnp.where(place == per_row * y, value, 0.0)
                return tuple(sums)

            start = (jnp.zeros((cap, cx), F32),) * cy
            sums = lax.fori_loop(0, peers, each, start, unroll=8)
            forcing = zero
            for y in range(cy):
                forcing = jnp.where(
                    sub == y, jnp.sum(sums[y], axis=0, keepdims=True), forcing
                )
            fld[0] = fld[0] + forcing * mask8

        return carry

    lax.fori_loop(0, NCPL, coupling, 0)

    for k in range(half):
        value = fld[k]
        out[k] = value[:cy]
        out[lev - 1 - k] = value[cy:]
    out[half] = fld[half][:cy]

    def finish(t, carry):
        ew_copy(t, 0).wait_send()
        ew_copy(t, 1).wait_send()

        if n_lat == 2:
            partner_copy(t, 0).wait_send()
            partner_copy(t, 1).wait_send()
        else:

            @pl.when(has_south)
            def _():
                ns_copy(t, 0).wait_send()

            @pl.when(has_north)
            def _():
                ns_copy(t, 1).wait_send()

        return carry

    lax.fori_loop(0, total, finish, 0)

    @pl.when(is_air)
    def _():
        dest_copy(s).wait_send()

        def done(c, carry):
            pltpu.make_async_copy(contrib.at[c], contrib.at[c], c_send.at[c]).wait()
            return carry

        lax.fori_loop(0, NCPL, done, 0)


def local(
    sizes, state, mixing, eastward, northward, sea_mask, weights, source_block, dest_block,
    record_counts,
):
    n_sec, n_lat, n_lon = sizes
    _, lev, cy, cx = state.shape
    blk, slots = weights.shape[3], weights.shape[5]
    peers, cap = source_block.shape[3:]
    half = lev // 2
    total = NCPL * NSUB
    groups = -(-(half + 1) // cy)
    if n_lat == 2:
        groups = -(-groups // 2)
    assert lev % 2 == 1 and 2 * (half + 1) <= cx and cx % blk == 0
    levels = (half + 1, 2 * cy, cx)
    vmem = pl.BlockSpec(memory_space=pltpu.VMEM)
    hbm = pl.BlockSpec(memory_space=pltpu.HBM)
    dma = pltpu.SemaphoreType.DMA
    result = pl.pallas_call(
        functools.partial(window, n_sec, n_lat, n_lon, cap),
        out_shape=jax.ShapeDtypeStruct((lev, cy, cx), F32),
        in_specs=[hbm] * 9,
        out_specs=vmem,
        scratch_shapes=[
            pltpu.VMEM((lev, cy, cx), F32),
            pltpu.VMEM((lev, cy, cx), mixing.dtype),
            pltpu.VMEM((lev, cy, cx), eastward.dtype),
            pltpu.VMEM((lev, cy, cx), northward.dtype),
            pltpu.VMEM((cy, cx), jnp.int32),
            pltpu.VMEM(weights.shape[3:], weights.dtype),
            pltpu.SMEM((cap, peers), jnp.int32),
            pltpu.SMEM((cap, peers), jnp.int32),
            pltpu.SMEM((1, peers), jnp.int32),
            dma((9,)),
        ]
        + [pltpu.VMEM(levels, F32)] * 7
        + [
            pltpu.VMEM((total, 2 * cy, cx), F32),
            pltpu.VMEM((total, 2, 2 * cy, cx), F32),
            pltpu.VMEM((total, 2, groups, 2 * cy, cx), F32),
            pltpu.VMEM((total, 2, groups, 2 * cy, cx), F32),
            pltpu.VMEM((blk, slots, cx), F32),
            pltpu.VMEM((slots, cx), jnp.int32),
            pltpu.VMEM((NCPL, peers, cap, cx), F32),
            pltpu.VMEM((NCPL, n_sec - 1, peers, cap, cx), F32),
            pltpu.VMEM((peers, cap, cx), jnp.int32),
            pltpu.VMEM((n_sec - 1, peers, cap, cx), jnp.int32),
            dma((total, 2)), dma((total, 2)), dma((total, 2)), dma((total, 2)),
            dma((NCPL,)), dma((NCPL,)), dma, dma((n_sec - 1,)),
        ],
        compiler_params=pltpu.CompilerParams(
            collective_id=0, has_side_effects=True, vmem_limit_bytes=63 * 1024 * 1024
        ),
    )(
        state[0], mixing[0], eastward[0], northward[0], sea_mask, weights[0, 0, 0],
        source_block[0, 0, 0].T, dest_block[0, 0, 0].T, record_counts[0, 0],
    )
    return result[None]


def solution(mesh):
    in_specs = (
        P("sec", None, "lat", "lon"),
        P("sec", None, "lat", "lon"),
        P("sec", None, "lat", "lon"),
        P("sec", None, "lat", "lon"),
        P("lat", "lon"),
        P("sec", "lat", "lon", None, None, None),
        P("sec", "lat", "lon", None, None),
        P("sec", "lat", "lon", None, None),
        P("sec", "lat", "lon", None),
    )
    out_specs = P("sec", None, "lat", "lon")
    sizes = tuple(mesh.shape[name] for name in ("sec", "lat", "lon"))
    return jax.shard_map(
        functools.partial(local, sizes), mesh=mesh, in_specs=in_specs, out_specs=out_specs,
        check_vma=False,
    )
```

```python
import functools

import jax
import jax.numpy as jnp
from jax import lax
from jax.experimental import pallas as pl
from jax.experimental.pallas import tpu as pltpu
from jax.sharding import PartitionSpec as P

NCPL = 4
NSUB = 2
MESH = pl.DeviceIdType.MESH
F32 = jnp.float32


def window(
    n_sec, n_lat, n_lon, cap, state_in, mixing_in, eastward_in, northward_in, sea_in, weights_in,
    source_in, dest_in_hbm, counts_in, out, state, mixing, eastward, northward, sea, weights, source,
    dest, counts, load_sem, fld, loc, coef, inv, low, east, north, ew_out, ew_in, ns_out, ns_in, table, rows_of,
    contrib, arrived, dest_out, dest_in, ew_send, ew_recv, ns_send, ns_recv, c_send, c_recv,
    d_send, d_recv,
):
    lev, cy, cx = state.shape
    half = lev // 2
    blk = weights.shape[0]
    slots = weights.shape[2]
    peers = n_lat * n_lon
    per_row = cx // blk
    groups = ns_out.shape[2]
    total = NCPL * NSUB

    s, a, o = lax.axis_index("sec"), lax.axis_index("lat"), lax.axis_index("lon")
    me = a * n_lon + o
    ocean = n_sec - 1
    is_ocean = s == ocean
    is_air = s != ocean
    to_east = (s, a, lax.rem(o + 1, n_lon))
    to_west = (s, a, lax.rem(o + n_lon - 1, n_lon))
    to_north = (s, a + 1, o)
    to_south = (s, a - 1, o)
    has_north = a < n_lat - 1
    has_south = a > 0

    loads = [
        pltpu.make_async_copy(src, dst, load_sem.at[i])
        for i, (src, dst) in enumerate(
            (
                (mixing_in, mixing), (state_in, state), (eastward_in, eastward),
                (northward_in, northward), (sea_in, sea), (weights_in, weights),
                (source_in, source), (dest_in_hbm, dest), (counts_in, counts),
            )
        )
    ]
    for load in loads:
        load.start()

    barrier = pltpu.get_barrier_semaphore()

    def greet(target):
        pl.semaphore_signal(barrier, inc=1, device_id=target, device_id_type=MESH)

    greet(to_east)
    greet(to_west)

    @pl.when(has_north)
    def _():
        greet(to_north)

    @pl.when(has_south)
    def _():
        greet(to_south)

    @pl.when(is_ocean)
    def _():
        def each(q, carry):
            for sec in range(n_sec - 1):
                greet((sec, q // n_lon, q % n_lon))
            return carry

        lax.fori_loop(0, peers, each, 0)

    lane = lax.broadcasted_iota(jnp.int32, (2 * cy, cx), 1)
    sub = lax.broadcasted_iota(jnp.int32, (2 * cy, cx), 0)
    row = sub % cy
    first_row, last_row = row == 0, row == cy - 1
    first_lane, last_lane = lane == 0, lane == cx - 1
    zero = jnp.zeros((2 * cy, cx), F32)

    def pair(ref, upper, lower):
        return jnp.concatenate([ref[upper].astype(F32), ref[lower].astype(F32)], axis=0)

    for load in loads[:5]:
        load.wait()

    mask4 = sea[...].astype(F32)
    mask8 = jnp.concatenate([mask4, mask4], axis=0)
    keep = jnp.where(is_ocean, mask8, jnp.ones_like(mask8))

    for k in range(half + 1):
        fld[k] = pair(state, k, lev - 1 - k)
        east[k] = 0.5 * pair(eastward, k, lev - 1 - k)
        north[k] = 0.5 * pair(northward, k, lev - 1 - k)

    outer = zero
    held = zero
    for k in range(half):
        inner = pair(mixing, k + 1, lev - 1 - k)
        grown = 1.0 + outer * held
        inverse = 1.0 / (grown + inner)
        inv[k] = inverse
        low[k] = outer * inverse
        coef[k] = inner * inverse
        held = grown * inverse
        outer = inner
    joined = outer * held
    inv[half] = 1.0 / (1.0 + joined + pltpu.roll(joined, cy, 0))
    low[half] = outer

    if n_lat != 2:

        @pl.when(jnp.logical_not(has_north))
        def _():
            ns_in[:, 0] = jnp.zeros((total, groups, 2 * cy, cx), F32)

        @pl.when(jnp.logical_not(has_south))
        def _():
            ns_in[:, 1] = jnp.zeros((total, groups, 2 * cy, cx), F32)

    lane_s = lax.broadcasted_iota(jnp.int32, (slots, cx), 1)

    waits = 2 + has_north.astype(jnp.int32) + has_south.astype(jnp.int32)
    waits = waits + jnp.where(is_air, peers, 0)
    pl.semaphore_wait(barrier, waits)

    def dest_copy(sec):
        return pltpu.make_async_remote_copy(
            src_ref=dest_out, dst_ref=dest_in.at[sec], send_sem=d_send, recv_sem=d_recv.at[sec],
            device_id=(ocean, a, o), device_id_type=MESH,
        )

    def prepare_records():
        for load in loads[5:]:
            load.wait()
        lane1 = lax.broadcasted_iota(jnp.int32, (1, cx), 1)
        for z in range(slots):
            rows_of[z : z + 1, :] = jnp.full((1, cx), source[z % cap, z // cap], jnp.int32)
        blocks = rows_of[...]
        here = (lane_s // blk) == (blocks % per_row)
        rows_of[...] = blocks // per_row
        spread = (
            lax.broadcasted_iota(jnp.int32, (blk, cx), 1) % blk
            == lax.broadcasted_iota(jnp.int32, (blk, cx), 0)
        ).astype(F32).astype(jnp.bfloat16)
        for d in range(blk):
            wide = lax.dot_general(
                weights[d], spread, (((0,), (0,)), ((), ())), preferred_element_type=F32
            )
            table[d] = jnp.where(here, wide, 0.0)
        slot_row = lax.broadcasted_iota(jnp.int32, (cap, cx), 0)
        for q in range(peers):
            value = jnp.full((cap, cx), dest[0, q], jnp.int32)
            for j in range(1, cap):
                value = jnp.where(slot_row == j, dest[j, q], value)
            dest_out[q] = jnp.where(slot_row < counts[0, q], value, -1)
        dest_copy(s).start()

    def ew_copy(t, way):
        return pltpu.make_async_remote_copy(
            src_ref=ew_out.at[t], dst_ref=ew_in.at[t, way], send_sem=ew_send.at[t, way],
            recv_sem=ew_recv.at[t, way], device_id=(to_west, to_east)[way], device_id_type=MESH,
        )

    def ns_copy(t, way):
        return pltpu.make_async_remote_copy(
            src_ref=ns_out.at[t, way], dst_ref=ns_in.at[t, way], send_sem=ns_send.at[t, way],
            recv_sem=ns_recv.at[t, way], device_id=(to_south, to_north)[way], device_id_type=MESH,
        )

    def partner_copy(t, piece):
        span = pl.ds(starts[piece], starts[piece + 1] - starts[piece])
        return pltpu.make_async_remote_copy(
            src_ref=ns_out.at[t, 0, span], dst_ref=ns_in.at[t, 0, span],
            send_sem=ns_send.at[t, piece], recv_sem=ns_recv.at[t, piece],
            device_id=(s, 1 - a, o), device_id_type=MESH,
        )

    starts = (0, 3 * groups // 10, 7 * groups // 10, groups)
    facing = (cy - 1) * (1 - a)
    facing_row = row == facing
    facing_sign = jnp.where(a == 0, 1.0, -1.0).astype(F32)

    def substep(right, t, meanwhile):
        partial = []
        running = None
        for k in range(half):
            scaled = right(k) * inv[k]
            running = scaled if k == 0 else scaled + low[k] * running
            partial.append(running)
        meet = low[half] * running
        solved = [None] * (half + 1)
        solved[half] = (right(half) + (meet + pltpu.roll(meet, cy, 0))) * inv[half]
        for k in reversed(range(half)):
            solved[k] = partial[k] + coef[k] * solved[k + 1]

        packed = zero
        if n_lat == 2:
            for k in reversed(range(half + 1)):
                g, j = k // cy, k % cy
                flux = pltpu.roll(
                    north[k] * solved[k], lax.rem(j + 2 * cy - facing, 2 * cy), 0
                )
                group = jnp.where(row == j, flux, zero if k == half or j == cy - 1 else group)
                flux = pltpu.roll(east[k] * solved[k], 2 * k + 1, 1)
                packed = jnp.where((lane // 2) == k, flux, packed)
                if j == 0:
                    ns_out[t, 0, g] = group
                    if g == starts[2]:
                        partner_copy(t, 2).start()
        else:
            southward = [zero] * groups
            northbound = [zero] * groups
            for k in reversed(range(half + 1)):
                flux = north[k] * solved[k]
                g, j = k // cy, k % cy
                here = row == j
                down = flux if j == 0 else pltpu.roll(flux, j, 0)
                up = flux if j == cy - 1 else pltpu.roll(flux, j + cy + 1, 0)
                southward[g] = jnp.where(here, down, southward[g])
                northbound[g] = jnp.where(here, up, northbound[g])
                if j == 0:
                    ns_out[t, 0, g] = southward[g]
                    ns_out[t, 1, g] = northbound[g]

            @pl.when(has_south)
            def _():
                ns_copy(t, 0).start()

            @pl.when(has_north)
            def _():
                ns_copy(t, 1).start()

            for k in range(half + 1):
                flux = pltpu.roll(east[k] * solved[k], 2 * k + 1, 1)
                packed = jnp.where((lane // 2) == k, flux, packed)
        ew_out[t] = packed
        ew_copy(t, 0).start()
        ew_copy(t, 1).start()
        if n_lat == 2:
            partner_copy(t, 0).start()
            partner_copy(t, 1).start()
        meanwhile()

        for k in range(half + 1):
            flux = east[k] * solved[k]
            across = jnp.where(last_lane, 0.0, pltpu.roll(flux, cx - 1, 1)) - jnp.where(
                first_lane, 0.0, pltpu.roll(flux, 1, 1)
            )
            flux = north[k] * solved[k]
            along = jnp.where(last_row, 0.0, pltpu.roll(flux, 2 * cy - 1, 0)) - jnp.where(
                first_row, 0.0, pltpu.roll(flux, 1, 0)
            )
            loc[k] = solved[k] + (across + along)

        ew_copy(t, 0).wait_recv()
        ew_copy(t, 1).wait_recv()

        if n_lat == 2:
            partner_copy(t, 2).wait_recv()
        else:

            @pl.when(has_north)
            def _():
                ns_copy(t, 0).wait_recv()

            @pl.when(has_south)
            def _():
                ns_copy(t, 1).wait_recv()

        from_east, from_west = ew_in[t, 0], ew_in[t, 1]
        sides = jnp.where(
            lane % 2 == 0, pltpu.roll(from_east, cx - 1, 1), -pltpu.roll(from_west, 1, 1)
        )
        edge = jnp.logical_or(first_lane, last_lane)
        group = None

        def complete(k):
            nonlocal group
            g, j = k // cy, k % cy
            beside = jnp.where(edge, pltpu.roll(sides, cx - (2 * k + 1), 1), 0.0)
            if n_lat == 2:
                if j == 0:
                    if g in starts[:2]:
                        partner_copy(t, starts.index(g)).wait_recv()
                    group = ns_in[t, 0, g] * facing_sign
                beyond = pltpu.roll(group, lax.rem(facing + 2 * cy - j, 2 * cy), 0)
                beyond = jnp.where(facing_row, beyond, 0.0)
            else:
                above, below = ns_in[t, 0, g], ns_in[t, 1, g]
                if j != cy - 1:
                    above = pltpu.roll(above, cy - 1 - j, 0)
                if j != 0:
                    below = pltpu.roll(below, 2 * cy - j, 0)
                beyond = jnp.where(last_row, above, jnp.where(first_row, -below, 0.0))
            return (loc[k] + (beside + beyond)) * keep

        return complete

    def contrib_copy(c, p):
        return pltpu.make_async_remote_copy(
            src_ref=contrib.at[c, p], dst_ref=arrived.at[c, jnp.minimum(s, ocean - 1), me],
            send_sem=c_send.at[c], recv_sem=c_recv.at[c],
            device_id=(ocean, p // n_lon, p % n_lon), device_id_type=MESH,
        )

    def send_records(c):
        surface = fld[0][cy:, :]
        picked = jnp.zeros((slots, cx), F32)
        for y in range(cy):
            picked = jnp.where(
                rows_of[...] == y, jnp.broadcast_to(surface[y : y + 1], (slots, cx)), picked
            )
        given = jnp.zeros((slots, cx), F32)
        for d in range(blk):
            value = jnp.sum(picked * table[d], axis=1, keepdims=True)
            given = jnp.where(lane_s % blk == d, value, given)
        for p in range(peers):
            contrib[c, p] = given[p * cap : (p + 1) * cap, :]

        def each(p, carry):
            contrib_copy(c, p).start()
            return carry

        lax.fori_loop(0, peers, each, 0)

    def nothing():
        pass

    def first_flight(c):
        pl.when(jnp.logical_and(is_air, c == 0))(prepare_records)

        @pl.when(jnp.logical_and(is_air, c >= 2))
        def _():
            send_records(c - 1)

    def coupling(c, carry):
        def right(k):
            return fld[k]

        for repeat in range(NSUB):
            right = substep(
                right, NSUB * c + repeat, functools.partial(first_flight, c) if repeat == 0 else nothing
            )
        for k in range(half + 1):
            fld[k] = right(k)

        @pl.when(jnp.logical_and(is_air, jnp.logical_or(c == 0, c == NCPL - 1)))
        def _():
            send_records(c)

        @pl.when(is_ocean)
        def _():
            @pl.when(c == 0)
            def _():
                for sec in range(n_sec - 1):
                    dest_copy(sec).wait_recv()

            pltpu.make_async_copy(arrived.at[c], arrived.at[c], c_recv.at[c]).wait()
            group = lax.broadcasted_iota(jnp.int32, (cap, cx), 1) // blk

            def each(q, sums):
                sums = list(sums)
                for sec in range(n_sec - 1):
                    place = dest_in[sec, q] - group
                    value = arrived[c, sec, q]
                    for y in range(cy):
                        sums[y] = sums[y] + jnp.where(place == per_row * y, value, 0.0)
                return tuple(sums)

            start = (jnp.zeros((cap, cx), F32),) * cy
            sums = lax.fori_loop(0, peers, each, start, unroll=8)
            forcing = zero
            for y in range(cy):
                forcing = jnp.where(
                    sub == y, jnp.sum(sums[y], axis=0, keepdims=True), forcing
                )
            fld[0] = fld[0] + forcing * mask8

        return carry

    lax.fori_loop(0, NCPL, coupling, 0)

    for k in range(half):
        value = fld[k]
        out[k] = value[:cy]
        out[lev - 1 - k] = value[cy:]
    out[half] = fld[half][:cy]

    def finish(t, carry):
        ew_copy(t, 0).wait_send()
        ew_copy(t, 1).wait_send()

        if n_lat == 2:
            for piece in range(3):
                partner_copy(t, piece).wait_send()
        else:

            @pl.when(has_south)
            def _():
                ns_copy(t, 0).wait_send()

            @pl.when(has_north)
            def _():
                ns_copy(t, 1).wait_send()

        return carry

    lax.fori_loop(0, total, finish, 0)

    @pl.when(is_ocean)
    def _():
        for load in loads[5:]:
            load.wait()

    @pl.when(is_air)
    def _():
        dest_copy(s).wait_send()

        def done(c, carry):
            pltpu.make_async_copy(contrib.at[c], contrib.at[c], c_send.at[c]).wait()
            return carry

        lax.fori_loop(0, NCPL, done, 0)


def local(
    sizes, state, mixing, eastward, northward, sea_mask, weights, source_block, dest_block,
    record_counts,
):
    n_sec, n_lat, n_lon = sizes
    _, lev, cy, cx = state.shape
    blk, slots = weights.shape[3], weights.shape[5]
    peers, cap = source_block.shape[3:]
    half = lev // 2
    total = NCPL * NSUB
    groups = -(-(half + 1) // cy)
    ways = 1 if n_lat == 2 else 2
    assert lev % 2 == 1 and 2 * (half + 1) <= cx and cx % blk == 0
    levels = (half + 1, 2 * cy, cx)
    vmem = pl.BlockSpec(memory_space=pltpu.VMEM)
    hbm = pl.BlockSpec(memory_space=pltpu.HBM)
    dma = pltpu.SemaphoreType.DMA
    result = pl.pallas_call(
        functools.partial(window, n_sec, n_lat, n_lon, cap),
        out_shape=jax.ShapeDtypeStruct((lev, cy, cx), F32),
        in_specs=[hbm] * 9,
        out_specs=vmem,
        scratch_shapes=[
            pltpu.VMEM((lev, cy, cx), F32),
            pltpu.VMEM((lev, cy, cx), mixing.dtype),
            pltpu.VMEM((lev, cy, cx), eastward.dtype),
            pltpu.VMEM((lev, cy, cx), northward.dtype),
            pltpu.VMEM((cy, cx), jnp.int32),
            pltpu.VMEM(weights.shape[3:], weights.dtype),
            pltpu.SMEM((cap, peers), jnp.int32),
            pltpu.SMEM((cap, peers), jnp.int32),
            pltpu.SMEM((1, peers), jnp.int32),
            dma((9,)),
        ]
        + [pltpu.VMEM(levels, F32)] * 7
        + [
            pltpu.VMEM((total, 2 * cy, cx), F32),
            pltpu.VMEM((total, 2, 2 * cy, cx), F32),
            pltpu.VMEM((total, ways, groups, 2 * cy, cx), F32),
            pltpu.VMEM((total, ways, groups, 2 * cy, cx), F32),
            pltpu.VMEM((blk, slots, cx), F32),
            pltpu.VMEM((slots, cx), jnp.int32),
            pltpu.VMEM((NCPL, peers, cap, cx), F32),
            pltpu.VMEM((NCPL, n_sec - 1, peers, cap, cx), F32),
            pltpu.VMEM((peers, cap, cx), jnp.int32),
            pltpu.VMEM((n_sec - 1, peers, cap, cx), jnp.int32),
            dma((total, 2)), dma((total, 2)), dma((total, 3)), dma((total, 3)),
            dma((NCPL,)), dma((NCPL,)), dma, dma((n_sec - 1,)),
        ],
        compiler_params=pltpu.CompilerParams(
            collective_id=0, has_side_effects=True, vmem_limit_bytes=63 * 1024 * 1024
        ),
    )(
        state[0], mixing[0], eastward[0], northward[0], sea_mask, weights[0, 0, 0],
        source_block[0, 0, 0].T, dest_block[0, 0, 0].T, record_counts[0, 0],
    )
    return result[None]


def solution(mesh):
    in_specs = (
        P("sec", None, "lat", "lon"),
        P("sec", None, "lat", "lon"),
        P("sec", None, "lat", "lon"),
        P("sec", None, "lat", "lon"),
        P("lat", "lon"),
        P("sec", "lat", "lon", None, None, None),
        P("sec", "lat", "lon", None, None),
        P("sec", "lat", "lon", None, None),
        P("sec", "lat", "lon", None),
    )
    out_specs = P("sec", None, "lat", "lon")
    sizes = tuple(mesh.shape[name] for name in ("sec", "lat", "lon"))
    return jax.shard_map(
        functools.partial(local, sizes), mesh=mesh, in_specs=in_specs, out_specs=out_specs,
        check_vma=False,
    )
```

```python
import functools

import jax
import jax.numpy as jnp
from jax import lax
from jax.experimental import pallas as pl
from jax.experimental.pallas import tpu as pltpu
from jax.sharding import PartitionSpec as P

NCPL = 4
NSUB = 2
MESH = pl.DeviceIdType.MESH
F32 = jnp.float32


def window(
    n_sec, n_lat, n_lon, cap, state_in, mixing_in, eastward_in, northward_in, sea_in, weights_in,
    source_in, dest_in_hbm, counts_in, out, state, mixing, eastward, northward, sea, weights, source,
    dest, counts, load_sem, fld, loc, coef, inv, low, east, north, ew_out, ew_in, ns_out, ns_in, table, rows_of,
    contrib, arrived, dest_out, dest_in, ew_send, ew_recv, ns_send, ns_recv, c_send, c_recv,
    d_send, d_recv,
):
    lev, cy, cx = state.shape
    half = lev // 2
    blk = weights.shape[0]
    slots = weights.shape[2]
    peers = n_lat * n_lon
    per_row = cx // blk
    groups = ns_out.shape[2]
    total = NCPL * NSUB

    s, a, o = lax.axis_index("sec"), lax.axis_index("lat"), lax.axis_index("lon")
    me = a * n_lon + o
    ocean = n_sec - 1
    is_ocean = s == ocean
    is_air = s != ocean
    to_east = (s, a, lax.rem(o + 1, n_lon))
    to_west = (s, a, lax.rem(o + n_lon - 1, n_lon))
    to_north = (s, a + 1, o)
    to_south = (s, a - 1, o)
    has_north = a < n_lat - 1
    has_south = a > 0

    loads = [
        pltpu.make_async_copy(src, dst, load_sem.at[i])
        for i, (src, dst) in enumerate(
            (
                (mixing_in, mixing), (state_in, state), (eastward_in, eastward),
                (northward_in, northward), (sea_in, sea), (weights_in, weights),
                (source_in, source), (dest_in_hbm, dest), (counts_in, counts),
            )
        )
    ]
    for load in loads:
        load.start()

    barrier = pltpu.get_barrier_semaphore()

    def greet(target):
        pl.semaphore_signal(barrier, inc=1, device_id=target, device_id_type=MESH)

    greet(to_east)
    greet(to_west)

    @pl.when(has_north)
    def _():
        greet(to_north)

    @pl.when(has_south)
    def _():
        greet(to_south)

    @pl.when(is_ocean)
    def _():
        def each(q, carry):
            for sec in range(n_sec - 1):
                greet((sec, q // n_lon, q % n_lon))
            return carry

        lax.fori_loop(0, peers, each, 0)

    lane = lax.broadcasted_iota(jnp.int32, (2 * cy, cx), 1)
    sub = lax.broadcasted_iota(jnp.int32, (2 * cy, cx), 0)
    row = sub % cy
    first_row, last_row = row == 0, row == cy - 1
    first_lane, last_lane = lane == 0, lane == cx - 1
    zero = jnp.zeros((2 * cy, cx), F32)

    def pair(ref, upper, lower):
        return jnp.concatenate([ref[upper].astype(F32), ref[lower].astype(F32)], axis=0)

    for load in loads[:5]:
        load.wait()

    mask4 = sea[...].astype(F32)
    mask8 = jnp.concatenate([mask4, mask4], axis=0)
    keep = jnp.where(is_ocean, mask8, jnp.ones_like(mask8))

    for k in range(half + 1):
        fld[k] = pair(state, k, lev - 1 - k)
        east[k] = 0.5 * pair(eastward, k, lev - 1 - k)
        north[k] = 0.5 * pair(northward, k, lev - 1 - k)

    outer = zero
    held = zero
    for k in range(half):
        inner = pair(mixing, k + 1, lev - 1 - k)
        grown = 1.0 + outer * held
        inverse = 1.0 / (grown + inner)
        inv[k] = inverse
        low[k] = outer * inverse
        coef[k] = inner * inverse
        held = grown * inverse
        outer = inner
    joined = outer * held
    inv[half] = 1.0 / (1.0 + joined + pltpu.roll(joined, cy, 0))
    low[half] = outer

    if n_lat != 2:

        @pl.when(jnp.logical_not(has_north))
        def _():
            ns_in[:, 0] = jnp.zeros((total, groups, 2 * cy, cx), F32)

        @pl.when(jnp.logical_not(has_south))
        def _():
            ns_in[:, 1] = jnp.zeros((total, groups, 2 * cy, cx), F32)

    lane_s = lax.broadcasted_iota(jnp.int32, (slots, cx), 1)

    waits = 2 + has_north.astype(jnp.int32) + has_south.astype(jnp.int32)
    waits = waits + jnp.where(is_air, peers, 0)
    pl.semaphore_wait(barrier, waits)

    def dest_copy(sec):
        return pltpu.make_async_remote_copy(
            src_ref=dest_out, dst_ref=dest_in.at[sec], send_sem=d_send, recv_sem=d_recv.at[sec],
            device_id=(ocean, a, o), device_id_type=MESH,
        )

    def prepare_records():
        for load in loads[5:]:
            load.wait()
        lane1 = lax.broadcasted_iota(jnp.int32, (1, cx), 1)
        for z in range(slots):
            rows_of[z : z + 1, :] = jnp.full((1, cx), source[z % cap, z // cap], jnp.int32)
        blocks = rows_of[...]
        here = (lane_s // blk) == (blocks % per_row)
        rows_of[...] = blocks // per_row
        spread = (
            lax.broadcasted_iota(jnp.int32, (blk, cx), 1) % blk
            == lax.broadcasted_iota(jnp.int32, (blk, cx), 0)
        ).astype(F32).astype(jnp.bfloat16)
        for d in range(blk):
            wide = lax.dot_general(
                weights[d], spread, (((0,), (0,)), ((), ())), preferred_element_type=F32
            )
            table[d] = jnp.where(here, wide, 0.0)
        slot = (lane1 // blk) % cap
        for q in range(peers):
            value = jnp.full((1, cx), dest[0, q], jnp.int32)
            for j in range(1, cap):
                value = jnp.where(slot == j, dest[j, q], value)
            dest_out[q : q + 1, :] = jnp.where(slot < counts[0, q], value, -1)
        dest_copy(s).start()

    def ew_copy(t, way):
        return pltpu.make_async_remote_copy(
            src_ref=ew_out.at[t], dst_ref=ew_in.at[t, way], send_sem=ew_send.at[t, way],
            recv_sem=ew_recv.at[t, way], device_id=(to_west, to_east)[way], device_id_type=MESH,
        )

    def ns_copy(t, way):
        return pltpu.make_async_remote_copy(
            src_ref=ns_out.at[t, way], dst_ref=ns_in.at[t, way], send_sem=ns_send.at[t, way],
            recv_sem=ns_recv.at[t, way], device_id=(to_south, to_north)[way], device_id_type=MESH,
        )

    def partner_copy(t, piece):
        span = pl.ds(starts[piece], starts[piece + 1] - starts[piece])
        return pltpu.make_async_remote_copy(
            src_ref=ns_out.at[t, 0, span], dst_ref=ns_in.at[t, 0, span],
            send_sem=ns_send.at[t, piece], recv_sem=ns_recv.at[t, piece],
            device_id=(s, 1 - a, o), device_id_type=MESH,
        )

    starts = (0, 3 * groups // 10, 7 * groups // 10, groups)
    facing = (cy - 1) * (1 - a)
    facing_row = row == facing
    facing_sign = jnp.where(a == 0, 1.0, -1.0).astype(F32)

    def substep(right, t, meanwhile):
        partial = []
        running = None
        for k in range(half):
            scaled = right(k) * inv[k]
            running = scaled if k == 0 else scaled + low[k] * running
            partial.append(running)
        meet = low[half] * running
        solved = [None] * (half + 1)
        solved[half] = (right(half) + (meet + pltpu.roll(meet, cy, 0))) * inv[half]
        for k in reversed(range(half)):
            solved[k] = partial[k] + coef[k] * solved[k + 1]

        packed = zero
        if n_lat == 2:
            for k in reversed(range(half + 1)):
                g, j = k // cy, k % cy
                flux = pltpu.roll(
                    north[k] * solved[k], lax.rem(j + 2 * cy - facing, 2 * cy), 0
                )
                group = jnp.where(row == j, flux, zero if k == half or j == cy - 1 else group)
                flux = pltpu.roll(east[k] * solved[k], 2 * k + 1, 1)
                packed = jnp.where((lane // 2) == k, flux, packed)
                if j == 0:
                    ns_out[t, 0, g] = group
                    if g == starts[2]:
                        partner_copy(t, 2).start()
        else:
            southward = [zero] * groups
            northbound = [zero] * groups
            for k in reversed(range(half + 1)):
                flux = north[k] * solved[k]
                g, j = k // cy, k % cy
                here = row == j
                down = flux if j == 0 else pltpu.roll(flux, j, 0)
                up = flux if j == cy - 1 else pltpu.roll(flux, j + cy + 1, 0)
                southward[g] = jnp.where(here, down, southward[g])
                northbound[g] = jnp.where(here, up, northbound[g])
                if j == 0:
                    ns_out[t, 0, g] = southward[g]
                    ns_out[t, 1, g] = northbound[g]

            @pl.when(has_south)
            def _():
                ns_copy(t, 0).start()

            @pl.when(has_north)
            def _():
                ns_copy(t, 1).start()

            for k in range(half + 1):
                flux = pltpu.roll(east[k] * solved[k], 2 * k + 1, 1)
                packed = jnp.where((lane // 2) == k, flux, packed)
        ew_out[t] = packed
        ew_copy(t, 0).start()
        ew_copy(t, 1).start()
        if n_lat == 2:
            partner_copy(t, 0).start()
            partner_copy(t, 1).start()
        meanwhile()

        for k in range(half + 1):
            flux = east[k] * solved[k]
            across = jnp.where(last_lane, 0.0, pltpu.roll(flux, cx - 1, 1)) - jnp.where(
                first_lane, 0.0, pltpu.roll(flux, 1, 1)
            )
            flux = north[k] * solved[k]
            along = jnp.where(last_row, 0.0, pltpu.roll(flux, 2 * cy - 1, 0)) - jnp.where(
                first_row, 0.0, pltpu.roll(flux, 1, 0)
            )
            loc[k] = solved[k] + (across + along)

        ew_copy(t, 0).wait_recv()
        ew_copy(t, 1).wait_recv()

        if n_lat == 2:
            partner_copy(t, 2).wait_recv()
        else:

            @pl.when(has_north)
            def _():
                ns_copy(t, 0).wait_recv()

            @pl.when(has_south)
            def _():
                ns_copy(t, 1).wait_recv()

        from_east, from_west = ew_in[t, 0], ew_in[t, 1]
        sides = jnp.where(
            lane % 2 == 0, pltpu.roll(from_east, cx - 1, 1), -pltpu.roll(from_west, 1, 1)
        )
        edge = jnp.logical_or(first_lane, last_lane)
        group = None

        def complete(k):
            nonlocal group
            g, j = k // cy, k % cy
            beside = jnp.where(edge, pltpu.roll(sides, cx - (2 * k + 1), 1), 0.0)
            if n_lat == 2:
                if j == 0:
                    if g in starts[:2]:
                        partner_copy(t, starts.index(g)).wait_recv()
                    group = ns_in[t, 0, g] * facing_sign
                beyond = pltpu.roll(group, lax.rem(facing + 2 * cy - j, 2 * cy), 0)
                beyond = jnp.where(facing_row, beyond, 0.0)
            else:
                above, below = ns_in[t, 0, g], ns_in[t, 1, g]
                if j != cy - 1:
                    above = pltpu.roll(above, cy - 1 - j, 0)
                if j != 0:
                    below = pltpu.roll(below, 2 * cy - j, 0)
                beyond = jnp.where(last_row, above, jnp.where(first_row, -below, 0.0))
            return (loc[k] + (beside + beyond)) * keep

        return complete

    def contrib_copy(c, p):
        return pltpu.make_async_remote_copy(
            src_ref=contrib.at[c, pl.ds(p, 1)],
            dst_ref=arrived.at[c, jnp.minimum(s, ocean - 1), pl.ds(me, 1)],
            send_sem=c_send.at[c], recv_sem=c_recv.at[c],
            device_id=(ocean, p // n_lon, p % n_lon), device_id_type=MESH,
        )

    def send_records(c):
        surface = fld[0][cy:, :]
        picked = jnp.zeros((slots, cx), F32)
        for y in range(cy):
            picked = jnp.where(
                rows_of[...] == y, jnp.broadcast_to(surface[y : y + 1], (slots, cx)), picked
            )
        given = jnp.zeros((slots, cx), F32)
        for d in range(blk):
            value = jnp.sum(picked * table[d], axis=1, keepdims=True)
            given = jnp.where(lane_s % blk == d, value, given)
        slot_s = lax.broadcasted_iota(jnp.int32, (slots, cx), 0) % cap
        given = jnp.where((lane_s // blk) % cap == slot_s, given, 0.0)
        for p in range(peers):
            contrib[c, p : p + 1, :] = jnp.sum(
                given[p * cap : (p + 1) * cap, :], axis=0, keepdims=True
            )

        def each(p, carry):
            contrib_copy(c, p).start()
            return carry

        lax.fori_loop(0, peers, each, 0)

    def nothing():
        pass

    def first_flight(c):
        pl.when(jnp.logical_and(is_air, c == 0))(prepare_records)

        @pl.when(jnp.logical_and(is_air, c >= 2))
        def _():
            send_records(c - 1)

    def coupling(c, carry):
        def right(k):
            return fld[k]

        for repeat in range(NSUB):
            right = substep(
                right, NSUB * c + repeat, functools.partial(first_flight, c) if repeat == 0 else nothing
            )
        for k in range(half + 1):
            fld[k] = right(k)

        @pl.when(jnp.logical_and(is_air, jnp.logical_or(c == 0, c == NCPL - 1)))
        def _():
            send_records(c)

        @pl.when(is_ocean)
        def _():
            @pl.when(c == 0)
            def _():
                for sec in range(n_sec - 1):
                    dest_copy(sec).wait_recv()

            pltpu.make_async_copy(arrived.at[c], arrived.at[c], c_recv.at[c]).wait()
            group = lax.broadcasted_iota(jnp.int32, (peers, cx), 1) // blk
            sums = [jnp.zeros((peers, cx), F32)] * cy
            for sec in range(n_sec - 1):
                value, target = arrived[c, sec], dest_in[sec]
                for turn in range(cap):
                    if turn:
                        value = pltpu.roll(value, blk, 1)
                        target = pltpu.roll(target, blk, 1)
                    place = target - group
                    for y in range(cy):
                        sums[y] = sums[y] + jnp.where(place == per_row * y, value, 0.0)
            forcing = zero
            for y in range(cy):
                forcing = jnp.where(
                    sub == y, jnp.sum(sums[y], axis=0, keepdims=True), forcing
                )
            fld[0] = fld[0] + forcing * mask8

        return carry

    lax.fori_loop(0, NCPL, coupling, 0)

    for k in range(half):
        value = fld[k]
        out[k] = value[:cy]
        out[lev - 1 - k] = value[cy:]
    out[half] = fld[half][:cy]

    def finish(t, carry):
        ew_copy(t, 0).wait_send()
        ew_copy(t, 1).wait_send()

        if n_lat == 2:
            for piece in range(3):
                partner_copy(t, piece).wait_send()
        else:

            @pl.when(has_south)
            def _():
                ns_copy(t, 0).wait_send()

            @pl.when(has_north)
            def _():
                ns_copy(t, 1).wait_send()

        return carry

    lax.fori_loop(0, total, finish, 0)

    @pl.when(is_ocean)
    def _():
        for load in loads[5:]:
            load.wait()

    @pl.when(is_air)
    def _():
        dest_copy(s).wait_send()

        def done(c, carry):
            pltpu.make_async_copy(contrib.at[c], contrib.at[c], c_send.at[c]).wait()
            return carry

        lax.fori_loop(0, NCPL, done, 0)


def local(
    sizes, state, mixing, eastward, northward, sea_mask, weights, source_block, dest_block,
    record_counts,
):
    n_sec, n_lat, n_lon = sizes
    _, lev, cy, cx = state.shape
    blk, slots = weights.shape[3], weights.shape[5]
    peers, cap = source_block.shape[3:]
    half = lev // 2
    total = NCPL * NSUB
    groups = -(-(half + 1) // cy)
    ways = 1 if n_lat == 2 else 2
    assert lev % 2 == 1 and 2 * (half + 1) <= cx and cx % (blk * cap) == 0
    levels = (half + 1, 2 * cy, cx)
    vmem = pl.BlockSpec(memory_space=pltpu.VMEM)
    hbm = pl.BlockSpec(memory_space=pltpu.HBM)
    dma = pltpu.SemaphoreType.DMA
    result = pl.pallas_call(
        functools.partial(window, n_sec, n_lat, n_lon, cap),
        out_shape=jax.ShapeDtypeStruct((lev, cy, cx), F32),
        in_specs=[hbm] * 9,
        out_specs=vmem,
        scratch_shapes=[
            pltpu.VMEM((lev, cy, cx), F32),
            pltpu.VMEM((lev, cy, cx), mixing.dtype),
            pltpu.VMEM((lev, cy, cx), eastward.dtype),
            pltpu.VMEM((lev, cy, cx), northward.dtype),
            pltpu.VMEM((cy, cx), jnp.int32),
            pltpu.VMEM(weights.shape[3:], weights.dtype),
            pltpu.SMEM((cap, peers), jnp.int32),
            pltpu.SMEM((cap, peers), jnp.int32),
            pltpu.SMEM((1, peers), jnp.int32),
            dma((9,)),
        ]
        + [pltpu.VMEM(levels, F32)] * 7
        + [
            pltpu.VMEM((total, 2 * cy, cx), F32),
            pltpu.VMEM((total, 2, 2 * cy, cx), F32),
            pltpu.VMEM((total, ways, groups, 2 * cy, cx), F32),
            pltpu.VMEM((total, ways, groups, 2 * cy, cx), F32),
            pltpu.VMEM((blk, slots, cx), F32),
            pltpu.VMEM((slots, cx), jnp.int32),
            pltpu.VMEM((NCPL, peers, cx), F32),
            pltpu.VMEM((NCPL, n_sec - 1, peers, cx), F32),
            pltpu.VMEM((peers, cx), jnp.int32),
            pltpu.VMEM((n_sec - 1, peers, cx), jnp.int32),
            dma((total, 2)), dma((total, 2)), dma((total, 3)), dma((total, 3)),
            dma((NCPL,)), dma((NCPL,)), dma, dma((n_sec - 1,)),
        ],
        compiler_params=pltpu.CompilerParams(
            collective_id=0, has_side_effects=True, vmem_limit_bytes=63 * 1024 * 1024
        ),
    )(
        state[0], mixing[0], eastward[0], northward[0], sea_mask, weights[0, 0, 0],
        source_block[0, 0, 0].T, dest_block[0, 0, 0].T, record_counts[0, 0],
    )
    return result[None]


def solution(mesh):
    in_specs = (
        P("sec", None, "lat", "lon"),
        P("sec", None, "lat", "lon"),
        P("sec", None, "lat", "lon"),
        P("sec", None, "lat", "lon"),
        P("lat", "lon"),
        P("sec", "lat", "lon", None, None, None),
        P("sec", "lat", "lon", None, None),
        P("sec", "lat", "lon", None, None),
        P("sec", "lat", "lon", None),
    )
    out_specs = P("sec", None, "lat", "lon")
    sizes = tuple(mesh.shape[name] for name in ("sec", "lat", "lon"))
    return jax.shard_map(
        functools.partial(local, sizes), mesh=mesh, in_specs=in_specs, out_specs=out_specs,
        check_vma=False,
    )
```

```python
import functools

import jax
import jax.numpy as jnp
from jax import lax
from jax.experimental import pallas as pl
from jax.experimental.pallas import tpu as pltpu
from jax.sharding import PartitionSpec as P

NCPL = 4
NSUB = 2
MESH = pl.DeviceIdType.MESH
F32 = jnp.float32


def window(
    n_sec, n_lat, n_lon, cap, state_in, mixing_in, eastward_in, northward_in, sea_in, weights_in,
    source_in, dest_in_hbm, counts_in, out, state, mixing, eastward, northward, sea, weights, source,
    dest, counts, load_sem, fld, loc, coef, inv, low, east, north, ew_out, ew_in, ns_out, ns_in, table, rows_of,
    contrib, arrived, dest_out, dest_in, ew_send, ew_recv, ns_send, ns_recv, c_send, c_recv,
    d_send, d_recv,
):
    lev, cy, cx = state.shape
    half = lev // 2
    blk = weights.shape[0]
    slots = weights.shape[2]
    peers = n_lat * n_lon
    per_row = cx // blk
    groups = ns_out.shape[2]
    total = NCPL * NSUB

    s, a, o = lax.axis_index("sec"), lax.axis_index("lat"), lax.axis_index("lon")
    me = a * n_lon + o
    ocean = n_sec - 1
    is_ocean = s == ocean
    is_air = s != ocean
    to_east = (s, a, lax.rem(o + 1, n_lon))
    to_west = (s, a, lax.rem(o + n_lon - 1, n_lon))
    to_north = (s, a + 1, o)
    to_south = (s, a - 1, o)
    has_north = a < n_lat - 1
    has_south = a > 0

    loads = [
        pltpu.make_async_copy(src, dst, load_sem.at[i])
        for i, (src, dst) in enumerate(
            (
                (mixing_in, mixing), (state_in, state), (eastward_in, eastward),
                (northward_in, northward), (sea_in, sea), (weights_in, weights),
                (source_in, source), (dest_in_hbm, dest), (counts_in, counts),
            )
        )
    ]
    for load in loads:
        load.start()

    barrier = pltpu.get_barrier_semaphore()

    def greet(target):
        pl.semaphore_signal(barrier, inc=1, device_id=target, device_id_type=MESH)

    greet(to_east)
    greet(to_west)

    @pl.when(has_north)
    def _():
        greet(to_north)

    @pl.when(has_south)
    def _():
        greet(to_south)

    @pl.when(is_ocean)
    def _():
        def each(q, carry):
            for sec in range(n_sec - 1):
                greet((sec, q // n_lon, q % n_lon))
            return carry

        lax.fori_loop(0, peers, each, 0)

    lane = lax.broadcasted_iota(jnp.int32, (2 * cy, cx), 1)
    sub = lax.broadcasted_iota(jnp.int32, (2 * cy, cx), 0)
    row = sub % cy
    first_row, last_row = row == 0, row == cy - 1
    first_lane, last_lane = lane == 0, lane == cx - 1
    zero = jnp.zeros((2 * cy, cx), F32)

    def pair(ref, upper, lower):
        return jnp.concatenate([ref[upper].astype(F32), ref[lower].astype(F32)], axis=0)

    for load in loads[:5]:
        load.wait()

    mask4 = sea[...].astype(F32)
    mask8 = jnp.concatenate([mask4, mask4], axis=0)
    keep = jnp.where(is_ocean, mask8, jnp.ones_like(mask8))

    for k in range(half + 1):
        fld[k] = pair(state, k, lev - 1 - k)
        east[k] = 0.5 * pair(eastward, k, lev - 1 - k)
        north[k] = 0.5 * pair(northward, k, lev - 1 - k)

    outer = zero
    held = zero
    for k in range(half):
        inner = pair(mixing, k + 1, lev - 1 - k)
        grown = 1.0 + outer * held
        inverse = 1.0 / (grown + inner)
        inv[k] = inverse
        low[k] = outer * inverse
        coef[k] = inner * inverse
        held = grown * inverse
        outer = inner
    joined = outer * held
    inv[half] = 1.0 / (1.0 + joined + pltpu.roll(joined, cy, 0))
    low[half] = outer

    if n_lat != 2:

        @pl.when(jnp.logical_not(has_north))
        def _():
            ns_in[:, 0] = jnp.zeros((total, groups, 2 * cy, cx), F32)

        @pl.when(jnp.logical_not(has_south))
        def _():
            ns_in[:, 1] = jnp.zeros((total, groups, 2 * cy, cx), F32)

    lane_s = lax.broadcasted_iota(jnp.int32, (slots, cx), 1)

    waits = 2 + has_north.astype(jnp.int32) + has_south.astype(jnp.int32)
    waits = waits + jnp.where(is_air, peers, 0)
    pl.semaphore_wait(barrier, waits)

    def dest_copy(sec):
        return pltpu.make_async_remote_copy(
            src_ref=dest_out, dst_ref=dest_in.at[sec], send_sem=d_send, recv_sem=d_recv.at[sec],
            device_id=(ocean, a, o), device_id_type=MESH,
        )

    def prepare_records():
        for load in loads[5:]:
            load.wait()
        lane1 = lax.broadcasted_iota(jnp.int32, (1, cx), 1)
        for z in range(slots):
            rows_of[z : z + 1, :] = jnp.full((1, cx), source[z % cap, z // cap], jnp.int32)
        blocks = rows_of[...]
        here = (lane_s // blk) == (blocks % per_row)
        rows_of[...] = blocks // per_row
        spread = (
            lax.broadcasted_iota(jnp.int32, (blk, cx), 1) % blk
            == lax.broadcasted_iota(jnp.int32, (blk, cx), 0)
        ).astype(F32).astype(jnp.bfloat16)
        for d in range(blk):
            wide = lax.dot_general(
                weights[d], spread, (((0,), (0,)), ((), ())), preferred_element_type=F32
            )
            table[d] = jnp.where(here, wide, 0.0)
        slot_row = lax.broadcasted_iota(jnp.int32, (cap, cx), 0)
        for q in range(peers):
            value = jnp.full((cap, cx), dest[0, q], jnp.int32)
            for j in range(1, cap):
                value = jnp.where(slot_row == j, dest[j, q], value)
            dest_out[q] = jnp.where(slot_row < counts[0, q], value, -1)
        dest_copy(s).start()

    def ew_copy(t, way):
        return pltpu.make_async_remote_copy(
            src_ref=ew_out.at[t], dst_ref=ew_in.at[t, way], send_sem=ew_send.at[t, way],
            recv_sem=ew_recv.at[t, way], device_id=(to_west, to_east)[way], device_id_type=MESH,
        )

    def ns_copy(t, way):
        return pltpu.make_async_remote_copy(
            src_ref=ns_out.at[t, way], dst_ref=ns_in.at[t, way], send_sem=ns_send.at[t, way],
            recv_sem=ns_recv.at[t, way], device_id=(to_south, to_north)[way], device_id_type=MESH,
        )

    def partner_copy(t, piece):
        span = pl.ds(starts[piece], starts[piece + 1] - starts[piece])
        return pltpu.make_async_remote_copy(
            src_ref=ns_out.at[t, 0, span], dst_ref=ns_in.at[t, 0, span],
            send_sem=ns_send.at[t, piece], recv_sem=ns_recv.at[t, piece],
            device_id=(s, 1 - a, o), device_id_type=MESH,
        )

    starts = (0, 3 * groups // 10, 7 * groups // 10, groups)
    facing = (cy - 1) * (1 - a)
    facing_row = row == facing
    facing_sign = jnp.where(a == 0, 1.0, -1.0).astype(F32)

    def substep(right, t, meanwhile):
        partial = []
        running = None
        for k in range(half):
            scaled = right(k) * inv[k]
            running = scaled if k == 0 else scaled + low[k] * running
            partial.append(running)
        meet = low[half] * running
        solved = [None] * (half + 1)
        solved[half] = (right(half) + (meet + pltpu.roll(meet, cy, 0))) * inv[half]
        for k in reversed(range(half)):
            solved[k] = partial[k] + coef[k] * solved[k + 1]

        packed = zero
        if n_lat == 2:
            for k in reversed(range(half + 1)):
                g, j = k // cy, k % cy
                flux = pltpu.roll(
                    north[k] * solved[k], lax.rem(j + 2 * cy - facing, 2 * cy), 0
                )
                group = jnp.where(row == j, flux, zero if k == half or j == cy - 1 else group)
                flux = pltpu.roll(east[k] * solved[k], 2 * k + 1, 1)
                packed = jnp.where((lane // 2) == k, flux, packed)
                if j == 0:
                    ns_out[t, 0, g] = group
                    if g == starts[2]:
                        partner_copy(t, 2).start()
        else:
            southward = [zero] * groups
            northbound = [zero] * groups
            for k in reversed(range(half + 1)):
                flux = north[k] * solved[k]
                g, j = k // cy, k % cy
                here = row == j
                down = flux if j == 0 else pltpu.roll(flux, j, 0)
                up = flux if j == cy - 1 else pltpu.roll(flux, j + cy + 1, 0)
                southward[g] = jnp.where(here, down, southward[g])
                northbound[g] = jnp.where(here, up, northbound[g])
                if j == 0:
                    ns_out[t, 0, g] = southward[g]
                    ns_out[t, 1, g] = northbound[g]

            @pl.when(has_south)
            def _():
                ns_copy(t, 0).start()

            @pl.when(has_north)
            def _():
                ns_copy(t, 1).start()

            for k in range(half + 1):
                flux = pltpu.roll(east[k] * solved[k], 2 * k + 1, 1)
                packed = jnp.where((lane // 2) == k, flux, packed)
        ew_out[t] = packed
        ew_copy(t, 0).start()
        ew_copy(t, 1).start()
        if n_lat == 2:
            partner_copy(t, 0).start()
            partner_copy(t, 1).start()
        meanwhile()

        for k in range(half + 1):
            flux = east[k] * solved[k]
            across = jnp.where(last_lane, 0.0, pltpu.roll(flux, cx - 1, 1)) - jnp.where(
                first_lane, 0.0, pltpu.roll(flux, 1, 1)
            )
            flux = north[k] * solved[k]
            along = jnp.where(last_row, 0.0, pltpu.roll(flux, 2 * cy - 1, 0)) - jnp.where(
                first_row, 0.0, pltpu.roll(flux, 1, 0)
            )
            loc[k] = solved[k] + (across + along)

        ew_copy(t, 0).wait_recv()
        ew_copy(t, 1).wait_recv()

        if n_lat == 2:
            partner_copy(t, 2).wait_recv()
        else:

            @pl.when(has_north)
            def _():
                ns_copy(t, 0).wait_recv()

            @pl.when(has_south)
            def _():
                ns_copy(t, 1).wait_recv()

        from_east, from_west = ew_in[t, 0], ew_in[t, 1]
        sides = jnp.where(
            lane % 2 == 0, pltpu.roll(from_east, cx - 1, 1), -pltpu.roll(from_west, 1, 1)
        )
        edge = jnp.logical_or(first_lane, last_lane)
        group = None

        def complete(k):
            nonlocal group
            g, j = k // cy, k % cy
            beside = jnp.where(edge, pltpu.roll(sides, cx - (2 * k + 1), 1), 0.0)
            if n_lat == 2:
                if j == 0:
                    if g in starts[:2]:
                        partner_copy(t, starts.index(g)).wait_recv()
                    group = ns_in[t, 0, g] * facing_sign
                beyond = pltpu.roll(group, lax.rem(facing + 2 * cy - j, 2 * cy), 0)
                beyond = jnp.where(facing_row, beyond, 0.0)
            else:
                above, below = ns_in[t, 0, g], ns_in[t, 1, g]
                if j != cy - 1:
                    above = pltpu.roll(above, cy - 1 - j, 0)
                if j != 0:
                    below = pltpu.roll(below, 2 * cy - j, 0)
                beyond = jnp.where(last_row, above, jnp.where(first_row, -below, 0.0))
            return (loc[k] + (beside + beyond)) * keep

        return complete

    def contrib_copy(c, p):
        return pltpu.make_async_remote_copy(
            src_ref=contrib.at[c, p], dst_ref=arrived.at[c, jnp.minimum(s, ocean - 1), me],
            send_sem=c_send.at[c], recv_sem=c_recv.at[c],
            device_id=(ocean, p // n_lon, p % n_lon), device_id_type=MESH,
        )

    def send_records(c):
        surface = fld[0][cy:, :]
        picked = jnp.zeros((slots, cx), F32)
        for y in range(cy):
            picked = jnp.where(
                rows_of[...] == y, jnp.broadcast_to(surface[y : y + 1], (slots, cx)), picked
            )
        given = jnp.zeros((slots, cx), F32)
        for d in range(blk):
            value = jnp.sum(picked * table[d], axis=1, keepdims=True)
            given = jnp.where(lane_s % blk == d, value, given)
        for p in range(peers):
            contrib[c, p] = given[p * cap : (p + 1) * cap, :]

        def each(p, carry):
            contrib_copy(c, p).start()
            return carry

        if peers <= 8:
            for p in range(peers):
                contrib_copy(c, p).start()
        else:
            lax.fori_loop(0, peers, each, 0)

    def nothing():
        pass

    def first_flight(c):
        pl.when(jnp.logical_and(is_air, c == 0))(prepare_records)

        @pl.when(jnp.logical_and(is_air, c >= 2))
        def _():
            send_records(c - 1)

    def coupling(c, carry):
        def right(k):
            return fld[k]

        for repeat in range(NSUB):
            right = substep(
                right, NSUB * c + repeat, functools.partial(first_flight, c) if repeat == 0 else nothing
            )
        for k in range(half + 1):
            fld[k] = right(k)

        @pl.when(jnp.logical_and(is_air, jnp.logical_or(c == 0, c == NCPL - 1)))
        def _():
            send_records(c)

        @pl.when(is_ocean)
        def _():
            @pl.when(c == 0)
            def _():
                for sec in range(n_sec - 1):
                    dest_copy(sec).wait_recv()

            pltpu.make_async_copy(arrived.at[c], arrived.at[c], c_recv.at[c]).wait()
            group = lax.broadcasted_iota(jnp.int32, (cap, cx), 1) // blk

            def each(q, sums):
                sums = list(sums)
                for sec in range(n_sec - 1):
                    place = dest_in[sec, q] - group
                    value = arrived[c, sec, q]
                    for y in range(cy):
                        sums[y] = sums[y] + jnp.where(place == per_row * y, value, 0.0)
                return tuple(sums)

            start = (jnp.zeros((cap, cx), F32),) * cy
            sums = lax.fori_loop(0, peers, each, start, unroll=8)
            forcing = zero
            for y in range(cy):
                forcing = jnp.where(
                    sub == y, jnp.sum(sums[y], axis=0, keepdims=True), forcing
                )
            fld[0] = fld[0] + forcing * mask8

        return carry

    lax.fori_loop(0, NCPL, coupling, 0)

    for k in range(half):
        value = fld[k]
        out[k] = value[:cy]
        out[lev - 1 - k] = value[cy:]
    out[half] = fld[half][:cy]

    def finish(t, carry):
        ew_copy(t, 0).wait_send()
        ew_copy(t, 1).wait_send()

        if n_lat == 2:
            for piece in range(3):
                partner_copy(t, piece).wait_send()
        else:

            @pl.when(has_south)
            def _():
                ns_copy(t, 0).wait_send()

            @pl.when(has_north)
            def _():
                ns_copy(t, 1).wait_send()

        return carry

    lax.fori_loop(0, total, finish, 0)

    @pl.when(is_ocean)
    def _():
        for load in loads[5:]:
            load.wait()

    @pl.when(is_air)
    def _():
        dest_copy(s).wait_send()

        def done(c, carry):
            pltpu.make_async_copy(contrib.at[c], contrib.at[c], c_send.at[c]).wait()
            return carry

        lax.fori_loop(0, NCPL, done, 0)


def local(
    sizes, state, mixing, eastward, northward, sea_mask, weights, source_block, dest_block,
    record_counts,
):
    n_sec, n_lat, n_lon = sizes
    _, lev, cy, cx = state.shape
    blk, slots = weights.shape[3], weights.shape[5]
    peers, cap = source_block.shape[3:]
    half = lev // 2
    total = NCPL * NSUB
    groups = -(-(half + 1) // cy)
    ways = 1 if n_lat == 2 else 2
    assert lev % 2 == 1 and 2 * (half + 1) <= cx and cx % blk == 0
    levels = (half + 1, 2 * cy, cx)
    vmem = pl.BlockSpec(memory_space=pltpu.VMEM)
    hbm = pl.BlockSpec(memory_space=pltpu.HBM)
    dma = pltpu.SemaphoreType.DMA
    result = pl.pallas_call(
        functools.partial(window, n_sec, n_lat, n_lon, cap),
        out_shape=jax.ShapeDtypeStruct((lev, cy, cx), F32),
        in_specs=[hbm] * 9,
        out_specs=vmem,
        scratch_shapes=[
            pltpu.VMEM((lev, cy, cx), F32),
            pltpu.VMEM((lev, cy, cx), mixing.dtype),
            pltpu.VMEM((lev, cy, cx), eastward.dtype),
            pltpu.VMEM((lev, cy, cx), northward.dtype),
            pltpu.VMEM((cy, cx), jnp.int32),
            pltpu.VMEM(weights.shape[3:], weights.dtype),
            pltpu.SMEM((cap, peers), jnp.int32),
            pltpu.SMEM((cap, peers), jnp.int32),
            pltpu.SMEM((1, peers), jnp.int32),
            dma((9,)),
        ]
        + [pltpu.VMEM(levels, F32)] * 7
        + [
            pltpu.VMEM((total, 2 * cy, cx), F32),
            pltpu.VMEM((total, 2, 2 * cy, cx), F32),
            pltpu.VMEM((total, ways, groups, 2 * cy, cx), F32),
            pltpu.VMEM((total, ways, groups, 2 * cy, cx), F32),
            pltpu.VMEM((blk, slots, cx), F32),
            pltpu.VMEM((slots, cx), jnp.int32),
            pltpu.VMEM((NCPL, peers, cap, cx), F32),
            pltpu.VMEM((NCPL, n_sec - 1, peers, cap, cx), F32),
            pltpu.VMEM((peers, cap, cx), jnp.int32),
            pltpu.VMEM((n_sec - 1, peers, cap, cx), jnp.int32),
            dma((total, 2)), dma((total, 2)), dma((total, 3)), dma((total, 3)),
            dma((NCPL,)), dma((NCPL,)), dma, dma((n_sec - 1,)),
        ],
        compiler_params=pltpu.CompilerParams(
            collective_id=0, has_side_effects=True, vmem_limit_bytes=63 * 1024 * 1024
        ),
    )(
        state[0], mixing[0], eastward[0], northward[0], sea_mask, weights[0, 0, 0],
        source_block[0, 0, 0].T, dest_block[0, 0, 0].T, record_counts[0, 0],
    )
    return result[None]


def solution(mesh):
    in_specs = (
        P("sec", None, "lat", "lon"),
        P("sec", None, "lat", "lon"),
        P("sec", None, "lat", "lon"),
        P("sec", None, "lat", "lon"),
        P("lat", "lon"),
        P("sec", "lat", "lon", None, None, None),
        P("sec", "lat", "lon", None, None),
        P("sec", "lat", "lon", None, None),
        P("sec", "lat", "lon", None),
    )
    out_specs = P("sec", None, "lat", "lon")
    sizes = tuple(mesh.shape[name] for name in ("sec", "lat", "lon"))
    return jax.shard_map(
        functools.partial(local, sizes), mesh=mesh, in_specs=in_specs, out_specs=out_specs,
        check_vma=False,
    )
```
